256 devices in a mesh: member: 4 (over z_lo), lat: 64 (over z_hi, y, x, core).
Axes of the slice: x: 4, y: 4, z: 8 (z_hi: 2, z_lo: 4; z = z_hi * 4 + z_lo), core: 2. Of those that a mesh axis runs over, the one named last changes fastest.
Arguments:
- grid_input: bfloat16 [4, 384, 768, 256], P('member', 'lat'), may hold values from -6 to 6
- saved_mixed: bfloat16 [4, 384, 768, 256], P('member', 'lat'), may hold values from -6 to 6
- target: bfloat16 [384, 768, 256], P('lat'), may hold values from -6 to 6
- land_weight: int32 [384, 768], P('lat'), may hold values from 0 to 3
- mix_weight: bfloat16 [256, 256], replicated, may hold values from -0.375 to 0.375
- degree_gain: float32 [384], replicated, may hold values from 0.3 to 3
- up_weight: bfloat16 [256, 512], replicated, may hold values from -0.375 to 0.375
- down_weight: bfloat16 [512, 256], replicated, may hold values from -0.25 to 0.25
Outputs:
- grad_input: bfloat16 [4, 384, 768, 256], P('member', 'lat')
The draws below stay inside these ranges and needn't reach their ends.
All inputs are finite; a program needn't handle non-finite values.
Results may differ from the reference program's by a relative error of at most 0.015.
Values may be sent and summed in bfloat16 or wider, within the bound.
A program may use at most 128 MiB of HBM per device.

```python
import math
import jax
import jax.numpy as jnp
from jax import lax

LATITUDES = 384
LONGITUDES = 768
CHANNELS = 256
HIDDEN_UNITS = 512
WAVENUMBERS = 384
MEMBERS = 4


def touch_ends(result, own_key, low, high):
    longest = result.shape.index(max(result.shape))
    spots = []
    for shift in (0, 1):
        where = [jax.random.randint(jax.random.fold_in(own_key, axis), (), 0, length) for axis, length in enumerate(result.shape)]
        where[longest] = (where[longest] + shift) % result.shape[longest]
        spots.append(tuple(where))
    return result.at[spots[0]].set(low).at[spots[1]].set(high)


def levels(own_key, shape, cuts, smallest, high):
    def one(dim, parts):
        heights = jax.random.uniform(jax.random.fold_in(jax.random.fold_in(own_key, 6), dim), (parts,), jnp.float32, smallest / len(cuts), high / len(cuts))
        return jnp.repeat(jnp.exp(heights), shape[dim] // parts).reshape((-1,) + (1,) * (len(shape) - dim - 1))

    factor_of = one(*cuts[0])
    for cut in cuts[1:]:
        factor_of = factor_of * one(*cut)
    return factor_of


def bell_draw(stream_key, shape, scale, reach, split=(), dtype=jnp.bfloat16):
    entries = jax.random.normal(stream_key, shape, jnp.float32) * scale
    if len(split) > 0:
        entries = levels(stream_key, shape, split, -0.22, 0.18) * entries
    return jnp.clip(entries, min=-reach, max=reach).astype(dtype)


def setup_inputs(seed: int = 0) -> dict:
    arg_keys = jax.random.split(jax.random.key(seed), 9)
    return {
        "grid_input": bell_draw(arg_keys[0], (MEMBERS, LATITUDES, LONGITUDES, CHANNELS), 1.0, 6.0, ((0, 4), (1, 64))),
        "saved_mixed": bell_draw(arg_keys[1], (MEMBERS, LATITUDES, LONGITUDES, CHANNELS), 1.0, 6.0, ((0, 4), (1, 64))),
        "target": bell_draw(arg_keys[2], (LATITUDES, LONGITUDES, CHANNELS), 1.0, 6.0, ((0, 64),)),
        "land_weight": touch_ends(jax.random.randint(arg_keys[3], (LATITUDES, LONGITUDES), 0, 4), jax.random.fold_in(arg_keys[3], 1), 0, 3).astype(jnp.int32),
        "mix_weight": bell_draw(arg_keys[4], (CHANNELS, CHANNELS), CHANNELS ** -0.5, 0.375),
        "degree_gain": jnp.clip(jnp.exp(jax.random.uniform(arg_keys[5], (LATITUDES,), jnp.float32, math.log(0.3), math.log(3.0))), 0.3, 3.0),
        "up_weight": bell_draw(arg_keys[6], (CHANNELS, HIDDEN_UNITS), CHANNELS ** -0.5, 0.375),
        "down_weight": bell_draw(arg_keys[7], (HIDDEN_UNITS, CHANNELS), HIDDEN_UNITS ** -0.5, 0.25),
    }


kappa_gelu = 0.7978845608
cubic_gelu = 0.044715
smooth_square = 0.25

def gelu_parts(inputs):
    tanh_part = jnp.tanh(kappa_gelu * (inputs + cubic_gelu * inputs * inputs * inputs))
    values = 0.5 * inputs * (1.0 + tanh_part)
    slopes = 0.5 * (1.0 + tanh_part) + 0.5 * inputs * (1.0 - tanh_part * tanh_part) * kappa_gelu * (1.0 + 3.0 * cubic_gelu * inputs * inputs)
    return (values, slopes)

def slope_abs(difference):
    return difference * lax.rsqrt(difference * difference + smooth_square)

def member_term(own_values, everyone, target, weights):
    member_count = everyone.shape[0]
    total = jnp.zeros(own_values.shape, jnp.float32)
    for slot in range(member_count):
        total = total + slope_abs(own_values - everyone[slot].astype(jnp.float32))
    direct = slope_abs(own_values - target.astype(jnp.float32))
    return (weights * (direct / member_count - total / (member_count * member_count))).astype(jnp.bfloat16)

def fourier_tables(lon_count, mode_count):
    positions = jnp.arange(lon_count)
    orders = jnp.arange(mode_count)
    phase = positions[:, None] * orders[None, :] % lon_count
    angle_grid = phase.astype(jnp.float32) * (2.0 * math.pi / lon_count)
    cosine = jnp.cos(angle_grid)
    sine = jnp.sin(angle_grid)
    factor = jnp.where(orders == 0, 1.0, 2.0).astype(jnp.float32)
    synth_table = jnp.concatenate([cosine * factor[None, :], -sine * factor[None, :]], axis=1).astype(jnp.bfloat16)
    analysis_table = jnp.concatenate([cosine.T, -sine.T], axis=0).astype(jnp.bfloat16)
    return (synth_table, analysis_table)

def legendre_table(orders, lat_count, degree_count):
    angles = (jnp.arange(lat_count).astype(jnp.float32) + 0.5) * (math.pi / lat_count)
    cosine = jnp.cos(angles)
    sine = jnp.sin(angles)
    order_f = orders.astype(jnp.float32)[:, None]
    factor_index = jnp.arange(1, lat_count + 1).astype(jnp.float32)
    ratios = jnp.log((2.0 * factor_index - 1.0) / (2.0 * factor_index))
    partial_log = lax.optimization_barrier(jnp.sum(jnp.where(factor_index[None, :] <= order_f, ratios[None, :], 0.0), axis=1))
    start_log = 0.5 * jnp.log(order_f + 0.5) + 0.5 * partial_log[:, None] + order_f * jnp.log(sine)[None, :]
    zeros_start = jnp.zeros((orders.shape[0], lat_count), jnp.float32)

    def advance(state, degree):
        older, newer, log_scale = state
        degree_f = degree.astype(jnp.float32)
        alpha_rec = jnp.sqrt(jnp.maximum(4.0 * degree_f * degree_f - 1.0, 1.0) / jnp.maximum(degree_f * degree_f - order_f * order_f, 1.0))
        below = degree_f - 1.0
        beta_rec = jnp.sqrt(jnp.maximum(below * below - order_f * order_f, 0.0) / jnp.maximum(4.0 * below * below - 1.0, 1.0))
        recurred = alpha_rec * (cosine[None, :] * newer - beta_rec * older)
        fresh = jnp.where(degree_f < order_f, 0.0, jnp.where(degree_f == order_f, 1.0, recurred))
        output = fresh * jnp.exp(log_scale)
        norm_value = jnp.where(degree_f < order_f, 1.0, jnp.maximum(jnp.abs(fresh), jnp.abs(newer)))
        return ((newer / norm_value, fresh / norm_value, log_scale + jnp.log(norm_value)), output)
    block_size = math.gcd(degree_count, 32)

    def advance_block(state, block_start):
        rows_out = []
        for offset in range(block_size):
            state, output = advance(state, block_start + offset)
            rows_out.append(output)
        return (state, jnp.stack(rows_out))
    start_state = (zeros_start, zeros_start, start_log + zeros_start)
    block_starts = (jnp.arange(degree_count // block_size) * block_size).astype(jnp.int32)
    final_state, table_blocks = lax.scan(advance_block, start_state, block_starts)
    return table_blocks.reshape(degree_count, orders.shape[0], lat_count)

def widen(array_low):
    return lax.optimization_barrier(array_low).astype(jnp.float32)

def mlp_branch(saved_one, up_weight, down_weight):
    flat_saved = saved_one.reshape(-1, saved_one.shape[-1])
    hidden_pre = jnp.dot(flat_saved, up_weight, preferred_element_type=jnp.float32)
    values, slopes = gelu_parts(hidden_pre)
    activation = values.astype(jnp.bfloat16)
    return (jnp.dot(activation, down_weight, preferred_element_type=jnp.float32), slopes)

def reference(grid_input, saved_mixed, target, land_weight, mix_weight, degree_gain, up_weight, down_weight):
    synth_table, analysis_table = fourier_tables(LONGITUDES, WAVENUMBERS)
    legendre = widen(legendre_table(jnp.arange(WAVENUMBERS), LATITUDES, LATITUDES).astype(jnp.bfloat16))
    angles = (jnp.arange(LATITUDES).astype(jnp.float32) + 0.5) * (math.pi / LATITUDES)
    quad_weight = jnp.sin(angles) * (math.pi / LATITUDES)
    weights = (jnp.sin(angles)[:, None] * land_weight.astype(jnp.float32))[:, :, None]

    def forward_member(pair):
        grid_one, saved_one = pair
        branch_out, unused_slopes = mlp_branch(saved_one, up_weight, down_weight)
        summed = grid_one.reshape(branch_out.shape).astype(jnp.float32) + branch_out
        return summed.astype(jnp.bfloat16).reshape(grid_one.shape)
    everyone = lax.map(forward_member, (grid_input, saved_mixed))
    cotangents = jnp.stack([member_term(everyone[slot].astype(jnp.float32), everyone, target, weights) for slot in range(MEMBERS)])

    def backward_member(pair):
        saved_one, cotangent = pair
        unused_branch, slopes = mlp_branch(saved_one, up_weight, down_weight)
        act_grad = jnp.dot(cotangent.reshape(-1, CHANNELS), down_weight.T, preferred_element_type=jnp.float32)
        pre_grad = (act_grad * slopes).astype(jnp.bfloat16)
        mixed_grad = jnp.dot(pre_grad, up_weight.T, preferred_element_type=jnp.float32).astype(jnp.bfloat16)
        mixed_grad = mixed_grad.reshape(LATITUDES, LONGITUDES, CHANNELS)
        wave_grad = jnp.einsum('jnc,nk->jkc', widen(mixed_grad), synth_table.astype(jnp.float32)).astype(jnp.bfloat16)
        wave_grad = wave_grad.reshape(LATITUDES, 2, WAVENUMBERS, CHANNELS)
        degree_grad = jnp.einsum('lmj,jpmc->lpmc', legendre, widen(wave_grad))
        gained = (degree_grad * degree_gain[:, None, None, None]).astype(jnp.bfloat16)
        coeff_grad = jnp.einsum('lpmd,cd->lpmc', widen(gained), mix_weight.astype(jnp.float32)).astype(jnp.bfloat16)
        lat_grad = jnp.einsum('lmj,lpmc->jpmc', legendre, widen(coeff_grad)) * quad_weight[:, None, None, None]
        lat_grad = lat_grad.astype(jnp.bfloat16).reshape(LATITUDES, 2 * WAVENUMBERS, CHANNELS)
        spatial = jnp.einsum('jkc,kn->jnc', widen(lat_grad), analysis_table.astype(jnp.float32)) * (1.0 / LONGITUDES)
        return (cotangent.astype(jnp.float32) + spatial).astype(jnp.bfloat16)
    return lax.map(backward_member, (saved_mixed, cotangents))
```

```python
import functools
import math

import jax
import jax.numpy as jnp
from jax import lax
from jax.experimental import pallas as pl
from jax.experimental.pallas import tpu as pltpu
from jax.sharding import PartitionSpec as P

kappa_gelu = 0.7978845608
cubic_gelu = 0.044715
smooth_square = 0.25


def gelu_parts(inputs):
    tanh_part = jnp.tanh(kappa_gelu * (inputs + cubic_gelu * inputs * inputs * inputs))
    values = 0.5 * inputs * (1.0 + tanh_part)
    slopes = 0.5 * (1.0 + tanh_part) + 0.5 * inputs * (1.0 - tanh_part * tanh_part) * kappa_gelu * (
        1.0 + 3.0 * cubic_gelu * inputs * inputs
    )
    return (values, slopes)


def slope_abs(difference):
    return difference * lax.rsqrt(difference * difference + smooth_square)


def member_terms(everyone, target, weights):
    member_count = everyone.shape[0]
    values = [everyone[slot].astype(jnp.float32) for slot in range(member_count)]
    totals = [jnp.zeros(target.shape, jnp.float32) for slot in range(member_count)]
    for first in range(member_count):
        for second in range(first + 1, member_count):
            slope = slope_abs(values[first] - values[second])
            totals[first] = totals[first] + slope
            totals[second] = totals[second] - slope
    wanted = target.astype(jnp.float32)
    terms = [
        weights
        * (slope_abs(values[slot] - wanted) / member_count - totals[slot] / (member_count * member_count))
        for slot in range(member_count)
    ]
    return jnp.stack(terms).astype(jnp.bfloat16)


def fourier_tables(lon_count, mode_count):
    positions = jnp.arange(lon_count)
    orders = jnp.arange(mode_count)
    phase = positions[:, None] * orders[None, :] % lon_count
    angle_grid = phase.astype(jnp.float32) * (2.0 * math.pi / lon_count)
    cosine = jnp.cos(angle_grid)
    sine = jnp.sin(angle_grid)
    factor = jnp.where(orders == 0, 1.0, 2.0).astype(jnp.float32)
    synth_table = jnp.concatenate(
        [cosine * factor[None, :], -sine * factor[None, :]], axis=1
    ).astype(jnp.bfloat16)
    analysis_table = jnp.concatenate([cosine.T, -sine.T], axis=0).astype(jnp.bfloat16)
    return (synth_table, analysis_table)


def legendre_kernel(block, start_ref, order_ref, cosine_ref, table_ref, rows_ref):
    degree_count = rows_ref.shape[0]
    order_count = table_ref.shape[0]
    order_f = order_ref[...]
    cosine = cosine_ref[...]
    zeros = jnp.zeros(cosine.shape, jnp.float32)

    def advance_block(step, state):
        older, newer, log_scale = state
        half_scale = jnp.exp(0.5 * log_scale)
        for offset in range(block):
            degree = step * block + offset
            degree_f = degree.astype(jnp.float32)
            below = degree_f - 1.0
            alpha_rec = jnp.sqrt(
                jnp.maximum(4.0 * degree_f * degree_f - 1.0, 1.0)
                / jnp.maximum(degree_f * degree_f - order_f * order_f, 1.0)
            )
            beta_rec = jnp.sqrt(
                jnp.maximum(below * below - order_f * order_f, 0.0)
                / jnp.maximum(4.0 * below * below - 1.0, 1.0)
            )
            recurred = alpha_rec * (cosine * newer - beta_rec * older)
            fresh = jnp.where(
                degree_f < order_f, 0.0, jnp.where(degree_f == order_f, 1.0, recurred)
            )
            rows_ref[degree] = (fresh * half_scale) * half_scale
            older, newer = newer, fresh
        largest = jnp.maximum(jnp.abs(older), jnp.abs(newer))
        norm_value = jnp.where(largest > 0.0, largest, 1.0)
        return (older / norm_value, newer / norm_value, log_scale + jnp.log(norm_value))

    lax.fori_loop(0, degree_count // block, advance_block, (zeros, zeros, start_ref[...]))
    for slot in range(order_count):
        table_ref[slot] = rows_ref[:, slot, :].astype(jnp.bfloat16)


def legendre_table(orders, angles, degree_count):
    cosine = jnp.cos(angles)
    sine = jnp.sin(angles)
    order_count = orders.shape[0]
    padded = (order_count + 7) // 8 * 8
    orders = jnp.concatenate([orders, jnp.broadcast_to(orders[:1], (padded - order_count,))])
    order_f = orders.astype(jnp.float32)[:, None]
    factor_index = jnp.arange(1, degree_count + 1).astype(jnp.float32)
    ratios = jnp.log((2.0 * factor_index - 1.0) / (2.0 * factor_index))
    partial_log = jnp.sum(jnp.where(factor_index[None, :] <= order_f, ratios[None, :], 0.0), axis=1)
    start_log = (
        0.5 * jnp.log(order_f + 0.5) + 0.5 * partial_log[:, None] + order_f * jnp.log(sine)[None, :]
    )
    shape = start_log.shape
    return pl.pallas_call(
        functools.partial(legendre_kernel, 16),
        out_shape=jax.ShapeDtypeStruct((order_count, degree_count, shape[1]), jnp.bfloat16),
        scratch_shapes=[pltpu.VMEM((degree_count,) + shape, jnp.float32)],
        compiler_params=pltpu.CompilerParams(vmem_limit_bytes=32 * 2**20),
    )(start_log, jnp.broadcast_to(order_f, shape), jnp.broadcast_to(cosine[None, :], shape))


def shards(
    grid_input, saved_mixed, target, land_weight, mix_weight, degree_gain, up_weight, down_weight
):
    rows_lat = grid_input.shape[1]
    lon_count = grid_input.shape[2]
    channel_count = grid_input.shape[3]
    total_lat = degree_gain.shape[0]
    mode_count = lon_count // 2
    local_modes = mode_count // lax.axis_size("lat")
    flat_saved = saved_mixed.reshape(rows_lat * lon_count, channel_count)
    hidden_pre = jnp.dot(flat_saved, up_weight, preferred_element_type=jnp.float32)
    values, slopes = gelu_parts(hidden_pre)
    activation = values.astype(jnp.bfloat16)
    branch_out = jnp.dot(activation, down_weight, preferred_element_type=jnp.float32)
    member_out = (grid_input.reshape(branch_out.shape).astype(jnp.float32) + branch_out).astype(
        jnp.bfloat16
    )
    member_out = member_out.reshape(rows_lat, lon_count, channel_count)
    lat_start = lax.axis_index("lat") * rows_lat
    local_angles = ((lat_start + jnp.arange(rows_lat)).astype(jnp.float32) + 0.5) * (
        math.pi / total_lat
    )
    weights = (jnp.sin(local_angles)[:, None] * land_weight.astype(jnp.float32))[:, :, None]
    member_count = lax.axis_size("member")
    part = lon_count // member_count
    part_start = lax.axis_index("member") * part
    everyone = lax.all_to_all(
        member_out.reshape(rows_lat, member_count, part, channel_count), "member", 1, 0
    )
    own_target = lax.dynamic_slice_in_dim(target, part_start, part, 1)
    own_weights = lax.dynamic_slice_in_dim(weights, part_start, part, 1)
    cotangent = member_terms(everyone, own_target, own_weights)
    cotangent = lax.all_to_all(cotangent, "member", 0, 1)
    cotangent = cotangent.reshape(rows_lat, lon_count, channel_count)
    act_grad = jnp.dot(
        cotangent.reshape(rows_lat * lon_count, channel_count),
        down_weight.T,
        preferred_element_type=jnp.float32,
    )
    pre_grad = (act_grad * slopes).astype(jnp.bfloat16)
    mixed_grad = jnp.dot(pre_grad, up_weight.T, preferred_element_type=jnp.float32).astype(
        jnp.bfloat16
    )
    mixed_grad = mixed_grad.reshape(rows_lat, lon_count, channel_count)
    synth_table, analysis_table = fourier_tables(lon_count, mode_count)
    wave_grad = jnp.einsum(
        "jnc,nk->jkc", mixed_grad, synth_table, preferred_element_type=jnp.float32
    ).astype(jnp.bfloat16)
    wave_grad = wave_grad.reshape(rows_lat, 2, mode_count, channel_count)
    wave_all = lax.all_to_all(wave_grad, "lat", split_axis=2, concat_axis=0, tiled=True)
    local_orders = lax.axis_index("lat") * local_modes + jnp.arange(local_modes)
    all_angles = (jnp.arange(total_lat).astype(jnp.float32) + 0.5) * (math.pi / total_lat)
    legendre = legendre_table(local_orders, all_angles, total_lat)
    quad_weight = jnp.sin(all_angles) * (math.pi / total_lat)
    degree_grad = jnp.einsum(
        "mlj,jpmc->lpmc", legendre, wave_all, preferred_element_type=jnp.float32
    )
    gained = (degree_grad * degree_gain[:, None, None, None]).astype(jnp.bfloat16)
    coeff_grad = jnp.einsum(
        "lpmd,cd->lpmc", gained, mix_weight, preferred_element_type=jnp.float32
    ).astype(jnp.bfloat16)
    lat_grad = (
        jnp.einsum("mlj,lpmc->jpmc", legendre, coeff_grad, preferred_element_type=jnp.float32)
        * quad_weight[:, None, None, None]
    )
    lat_grad = lat_grad.astype(jnp.bfloat16)
    returned = lax.all_to_all(lat_grad, "lat", split_axis=0, concat_axis=2, tiled=True)
    spatial = jnp.einsum(
        "jkc,kn->jnc",
        returned.reshape(rows_lat, 2 * mode_count, channel_count),
        analysis_table,
        preferred_element_type=jnp.float32,
    ) * (1.0 / lon_count)
    grad_input = (cotangent.astype(jnp.float32) + spatial).astype(jnp.bfloat16)
    return grad_input[None]


def solution(mesh):
    in_specs = (
        P("member", "lat", None, None),
        P("member", "lat", None, None),
        P("lat", None, None),
        P("lat", None),
        P(),
        P(),
        P(),
        P(),
    )
    out_specs = P("member", "lat", None, None)
    return jax.shard_map(shards, mesh=mesh, in_specs=in_specs, out_specs=out_specs, check_vma=False)
```

```python
import functools
import math

import jax
import jax.numpy as jnp
import ml_dtypes
import numpy as np
from jax import lax
from jax.experimental import pallas as pl
from jax.experimental.pallas import tpu as pltpu
from jax.sharding import PartitionSpec as P

kappa_gelu = 0.7978845608
cubic_gelu = 0.044715
smooth_square = 0.25
pair_rows = 2
MESH = pl.DeviceIdType.MESH


def gelu_parts(inputs):
    squared = inputs * inputs
    tanh_part = jnp.tanh(kappa_gelu * inputs * (1.0 + cubic_gelu * squared))
    half_sum = 0.5 * (1.0 + tanh_part)
    values = inputs * half_sum
    slopes = half_sum + 0.5 * inputs * (1.0 - tanh_part * tanh_part) * (
        kappa_gelu + (3.0 * cubic_gelu * kappa_gelu) * squared
    )
    return (values, slopes)


def slope_abs(difference):
    return difference * lax.rsqrt(difference * difference + smooth_square)


def dot_nn(lhs, rhs):
    return lax.dot_general(lhs, rhs, (((1,), (0,)), ((), ())), preferred_element_type=jnp.float32)


def dot_nt(lhs, rhs):
    return lax.dot_general(lhs, rhs, (((1,), (1,)), ((), ())), preferred_element_type=jnp.float32)


def dot_tn(lhs, rhs):
    return lax.dot_general(lhs, rhs, (((0,), (0,)), ((), ())), preferred_element_type=jnp.float32)


def fourier_tables(lon_count, plane_count, orders_each):
    mode_count = lon_count // 2
    orders = np.arange(mode_count).reshape(2, plane_count, orders_each)
    positions = np.arange(lon_count)
    phase = (orders[..., None] * positions) % lon_count
    angles = phase.astype(np.float32) * np.float32(2.0 * math.pi / lon_count)
    cosine = np.cos(angles)
    sine = np.sin(angles)
    factor = np.where(orders == 0, 1.0, 2.0).astype(np.float32)[..., None]
    half_rows = plane_count * orders_each * 2
    synth = np.stack([cosine * factor, -sine * factor], axis=3)
    synth = synth.reshape(2, half_rows, lon_count).astype(ml_dtypes.bfloat16)
    analysis = np.stack([cosine, -sine], axis=3)
    analysis = analysis.reshape(2, plane_count, orders_each // 2, 4, lon_count)
    analysis = analysis.transpose(0, 4, 2, 1, 3).reshape(2, lon_count, half_rows)
    return (jnp.asarray(synth), jnp.asarray(analysis.astype(ml_dtypes.bfloat16)))


def legendre_fill(block, start_ref, order_ref, cosine_ref, rows_ref, table_ref):
    degree_count = rows_ref.shape[0]
    order_f = order_ref[...]
    cosine = cosine_ref[...]
    zeros = jnp.zeros(cosine.shape, jnp.float32)

    def advance_block(step, state):
        older, newer, log_scale = state
        half_scale = jnp.exp(0.5 * log_scale)
        for offset in range(block):
            degree = step * block + offset
            degree_f = degree.astype(jnp.float32)
            below = degree_f - 1.0
            alpha_rec = jnp.sqrt(
                jnp.maximum(4.0 * degree_f * degree_f - 1.0, 1.0)
                / jnp.maximum(degree_f * degree_f - order_f * order_f, 1.0)
            )
            beta_rec = jnp.sqrt(
                jnp.maximum(below * below - order_f * order_f, 0.0)
                / jnp.maximum(4.0 * below * below - 1.0, 1.0)
            )
            recurred = alpha_rec * (cosine * newer - beta_rec * older)
            fresh = jnp.where(
                degree_f < order_f, 0.0, jnp.where(degree_f == order_f, 1.0, recurred)
            )
            rows_ref[degree] = (fresh * half_scale) * half_scale
            older, newer = newer, fresh
        largest = jnp.maximum(jnp.abs(older), jnp.abs(newer))
        norm_value = jnp.where(largest > 0.0, largest, 1.0)
        return (older / norm_value, newer / norm_value, log_scale + jnp.log(norm_value))

    lax.fori_loop(0, degree_count // block, advance_block, (zeros, zeros, start_ref[...]))
    for slot in range(table_ref.shape[0]):
        table_ref[slot] = rows_ref[:, slot, :].astype(jnp.bfloat16)


def legendre_start(orders, angles, degree_count):
    order_count = orders.shape[0]
    padded = (order_count + 7) // 8 * 8
    orders = jnp.concatenate([orders, jnp.broadcast_to(orders[:1], (padded - order_count,))])
    order_f = orders.astype(jnp.float32)[:, None]
    factor_index = jnp.arange(1, degree_count + 1).astype(jnp.float32)
    ratios = jnp.log((2.0 * factor_index - 1.0) / (2.0 * factor_index))
    partial_log = jnp.sum(jnp.where(factor_index[None, :] <= order_f, ratios[None, :], 0.0), axis=1)
    start_log = (
        0.5 * jnp.log(order_f + 0.5)
        + 0.5 * partial_log[:, None]
        + order_f * jnp.log(jnp.sin(angles))[None, :]
    )
    shape = start_log.shape
    return (
        start_log,
        jnp.broadcast_to(order_f, shape),
        jnp.broadcast_to(jnp.cos(angles)[None, :], shape),
    )


def fused_kernel(
    grid_ref, saved_ref, target_ref, weight_ref, mix_ref, gain_ref, up_ref, down_ref,
    synth_ref, analysis_ref, start_ref, order_ref, cosine_ref, quad_ref,
    out_ref,
    own_target, send_points, recv_points, send_cot, cot_ref, slopes_ref, mixed_ref,
    gather_f32, zsend, zrecv, psend, precv, wave_f32, rows_ref, table_ref, wave_ref,
    rsend, rrecv, yown, zsend_back, zrecv_back,
    target_sem, point_ss, point_rs, cot_ss, cot_rs, z_ss, z_rs, p_ss, p_rs, r_ss, r_rs,
    zb_ss, zb_rs,
):
    row_count, lon_count, channels = saved_ref.shape
    member_count = recv_points.shape[0]
    part = lon_count // member_count
    plane_count = precv.shape[0]
    pair_count = precv.shape[1]
    piece = precv.shape[2]
    orders_each = table_ref.shape[0]
    keys_each = 2 * orders_each
    chunk_count = rrecv.shape[0]
    chunk_keys = keys_each // chunk_count
    chunk_span = plane_count * chunk_keys
    row_slots = 2 * row_count

    member = lax.axis_index("member")
    lat = lax.axis_index("lat")
    half = lat // plane_count
    spot = lat - half * plane_count
    partner = {"lat": lax.rem(lat + plane_count, 2 * plane_count)}

    def member_peer(step):
        return {"member": lax.rem(member + step, member_count)}

    def plane_spot(step):
        return lax.rem(spot + step, plane_count)

    def plane_peer(step):
        return {"lat": half * plane_count + plane_spot(step)}

    target_copy = pltpu.make_async_copy(
        target_ref.at[:, pl.ds(member * part, part), :], own_target, target_sem
    )
    target_copy.start()

    barrier = pltpu.get_barrier_semaphore()
    for step in range(1, member_count):
        pl.semaphore_signal(barrier, inc=1, device_id=member_peer(step), device_id_type=MESH)
    pl.semaphore_signal(barrier, inc=1, device_id=partner, device_id_type=MESH)

    def greet(step, carry):
        pl.semaphore_signal(barrier, inc=1, device_id=plane_peer(step), device_id_type=MESH)
        return carry

    lax.fori_loop(1, plane_count, greet, 0)
    pl.semaphore_wait(barrier, member_count - 1 + 1 + plane_count - 1)

    def point_copy(row, step):
        return pltpu.make_async_remote_copy(
            src_ref=send_points.at[step - 1, row],
            dst_ref=recv_points.at[member_count - step, row],
            send_sem=point_ss.at[row, step - 1],
            recv_sem=point_rs.at[row, step - 1],
            device_id=member_peer(step),
            device_id_type=MESH,
        )

    def cot_copy(row, step):
        return pltpu.make_async_remote_copy(
            src_ref=send_cot.at[step - 1, row],
            dst_ref=cot_ref.at[row, pl.ds(member * part, part), :],
            send_sem=cot_ss.at[row, step - 1],
            recv_sem=cot_rs.at[row, step - 1],
            device_id=member_peer(step),
            device_id_type=MESH,
        )

    def z_copy(row):
        return pltpu.make_async_remote_copy(
            src_ref=zsend.at[row],
            dst_ref=zrecv.at[row],
            send_sem=z_ss.at[row],
            recv_sem=z_rs.at[row],
            device_id=partner,
            device_id_type=MESH,
        )

    def p_copy(pair, step):
        return pltpu.make_async_remote_copy(
            src_ref=psend.at[pair, plane_spot(step)],
            dst_ref=precv.at[spot, pair],
            send_sem=p_ss.at[pair, step],
            recv_sem=p_rs.at[pair, step],
            device_id=plane_peer(step),
            device_id_type=MESH,
        )

    def r_copy(chunk, step):
        return pltpu.make_async_remote_copy(
            src_ref=rsend.at[chunk, plane_spot(step)],
            dst_ref=rrecv.at[chunk, spot],
            send_sem=r_ss.at[chunk, step],
            recv_sem=r_rs.at[chunk, step],
            device_id=plane_peer(step),
            device_id_type=MESH,
        )

    def zb_copy(chunk):
        return pltpu.make_async_remote_copy(
            src_ref=zsend_back.at[:, pl.ds(chunk * chunk_span, chunk_span), :],
            dst_ref=zrecv_back.at[:, pl.ds(chunk * chunk_span, chunk_span), :],
            send_sem=zb_ss.at[chunk],
            recv_sem=zb_rs.at[chunk],
            device_id=partner,
            device_id_type=MESH,
        )

    def forward_part(row, step):
        begin = pl.multiple_of(lax.rem(member + step, member_count) * part, part)
        hidden_pre = dot_nn(saved_ref[row, pl.ds(begin, part), :], up_ref[...])
        values, slopes = gelu_parts(hidden_pre)
        slopes_ref[row, pl.ds(begin, part), :] = slopes.astype(jnp.bfloat16)
        branch = dot_nn(values.astype(jnp.bfloat16), down_ref[...])
        summed = grid_ref[row, pl.ds(begin, part), :].astype(jnp.float32) + branch
        return summed.astype(jnp.bfloat16)

    def forward_row(row):
        def one(step, carry):
            send_points[step - 1, row] = forward_part(row, step)
            point_copy(row, step).start()
            return carry

        lax.fori_loop(1, member_count, one, 0)
        recv_points[0, row] = forward_part(row, 0)

    strip = 16 if part % 16 == 0 else part

    def loss_row(row):
        for step in range(1, member_count):
            point_copy(row, step).wait_recv()
        own_begin = pl.multiple_of(member * part, part)

        def one(index, carry):
            begin = pl.multiple_of(index * strip, strip)
            here = pl.ds(begin, strip)
            values = [
                recv_points[slot, row, here, :].astype(jnp.float32) for slot in range(member_count)
            ]
            totals = [jnp.zeros(values[0].shape, jnp.float32) for slot in range(member_count)]
            for first in range(member_count):
                for second in range(first + 1, member_count):
                    slope = slope_abs(values[first] - values[second])
                    totals[first] = totals[first] + slope
                    totals[second] = totals[second] - slope
            wanted = own_target[row, here, :].astype(jnp.float32)
            weights = weight_ref[row, here, :]
            for slot in range(member_count):
                term = weights * (
                    slope_abs(values[slot] - wanted) / member_count
                    - totals[slot] / (member_count * member_count)
                )
                if slot == 0:
                    spot_here = pl.ds(pl.multiple_of(own_begin + begin, strip), strip)
                    cot_ref[row, spot_here, :] = term.astype(jnp.bfloat16)
                else:
                    send_cot[slot - 1, row, here, :] = term.astype(jnp.bfloat16)
            return carry

        lax.fori_loop(0, part // strip, one, 0)
        for step in range(1, member_count):
            cot_copy(row, step).start()

    blocks, lane_width = gather_f32.shape[0], gather_f32.shape[2]

    def lanes_of(block):
        return slice(block * lane_width, (block + 1) * lane_width)

    def scatter_rows(first, count, stride, values):
        for block in range(blocks):
            gather_f32[block, pl.ds(first, count, stride=stride), :] = values[:, lanes_of(block)]

    def backward_row(row, own_slot):
        for step in range(1, member_count):
            cot_copy(row, step).wait_recv()

        def one(index, carry):
            here = pl.ds(pl.multiple_of(index * part, part), part)
            act_grad = dot_nt(cot_ref[row, here, :], down_ref[...])
            pre_grad = (act_grad * slopes_ref[row, here, :].astype(jnp.float32)).astype(jnp.bfloat16)
            mixed_ref[here, :] = dot_nt(pre_grad, up_ref[...]).astype(jnp.bfloat16)
            return carry

        lax.fori_loop(0, member_count, one, 0)
        other = dot_nn(synth_ref[1 - half], mixed_ref[...])
        zsend[row] = other.astype(jnp.bfloat16)
        z_copy(row).start()
        own = dot_nn(synth_ref[half], mixed_ref[...])
        scatter_rows(own_slot, own.shape[0], 2 * pair_rows, own)

    def plane_pair(pair):
        for inner in range(pair_rows):
            row = pair * pair_rows + inner
            z_copy(row).wait_recv()
            scatter_rows(
                pair_rows + inner, zrecv.shape[1], 2 * pair_rows, zrecv[row].astype(jnp.float32)
            )
        for block in range(blocks):
            psend[pair, :, :, lanes_of(block)] = (
                gather_f32[block].reshape(plane_count, piece, lane_width).astype(jnp.bfloat16)
            )

        def one(step, carry):
            p_copy(pair, step).start()
            return carry

        lax.fori_loop(1, plane_count, one, 0)
        precv[spot, pair] = psend[pair, spot]

    forward_row(0)
    forward_row(1)
    legendre_fill(
        math.gcd(rows_ref.shape[0], 16), start_ref, order_ref, cosine_ref, rows_ref, table_ref
    )
    target_copy.wait()
    for row in range(row_count):
        loss_row(row)
        if row + 2 < row_count:
            forward_row(row + 2)
        if row >= 1:
            backward_row(row - 1, (row - 1) % pair_rows)
            if row % pair_rows == 0:
                plane_pair(row // pair_rows - 1)
    backward_row(row_count - 1, (row_count - 1) % pair_rows)
    plane_pair(pair_count - 1)

    def await_plane(step, carry):
        for pair in range(pair_count):
            p_copy(pair, step).wait_recv()
        return carry

    lax.fori_loop(1, plane_count, await_plane, 0)

    group = pair_count * piece

    def widen(index, carry):
        here = pl.ds(pl.multiple_of(index * group, group), group)
        for block in range(blocks):
            wave_f32[block, here, :] = (
                precv[index, :, :, lanes_of(block)].reshape(group, lane_width).astype(jnp.float32)
            )
        return carry

    lax.fori_loop(0, plane_count, widen, 0)
    slots_each = 2 * pair_rows

    def spectral_chunk(chunk):
        def one_order(inner, carry):
            order = chunk * (chunk_keys // 2) + inner
            for phase in range(2):
                key = order * 2 + phase
                for pair in range(pair_count):
                    for slot in range(slots_each):
                        first = pair * piece + key * slots_each + slot
                        begin = (pair * slots_each + slot) * plane_count
                        for block in range(blocks):
                            lane_begin = phase * channels + block * lane_width
                            wave_ref[
                                begin : begin + plane_count, lane_begin : lane_begin + lane_width
                            ] = wave_f32[block, pl.ds(first, plane_count, stride=group), :].astype(
                                jnp.bfloat16
                            )
            degree_grad = dot_nn(table_ref[order], wave_ref[...])
            gained = (degree_grad * gain_ref[...]).astype(jnp.bfloat16)
            coeff_grad = jnp.concatenate(
                [
                    dot_nt(gained[:, :channels], mix_ref[...]).astype(jnp.bfloat16),
                    dot_nt(gained[:, channels:], mix_ref[...]).astype(jnp.bfloat16),
                ],
                axis=1,
            )
            lat_grad = dot_tn(table_ref[order], coeff_grad) * quad_ref[...]
            for phase in range(2):
                for slot in range(row_slots):
                    first = (inner * 2 + phase) * row_slots + slot
                    scatter_rows(
                        first,
                        plane_count,
                        piece,
                        lat_grad[
                            slot * plane_count : (slot + 1) * plane_count,
                            phase * channels : (phase + 1) * channels,
                        ],
                    )
            return carry

        lax.fori_loop(0, chunk_keys // 2, one_order, 0)
        for block in range(blocks):
            rsend[chunk, :, :, lanes_of(block)] = (
                gather_f32[block].reshape(plane_count, piece, lane_width).astype(jnp.bfloat16)
            )

        def one(step, carry):
            r_copy(chunk, step).start()
            return carry

        lax.fori_loop(1, plane_count, one, 0)
        rrecv[chunk, spot] = rsend[chunk, spot]

    def return_chunk(chunk):
        def await_one(step, carry):
            r_copy(chunk, step).wait_recv()
            return carry

        lax.fori_loop(1, plane_count, await_one, 0)
        for block in range(blocks):
            gather_f32[block] = (
                rrecv[chunk, :, :, lanes_of(block)]
                .reshape(plane_count * piece, lane_width)
                .astype(jnp.float32)
            )
        here = pl.ds(chunk * chunk_span, chunk_span)
        for row in range(row_count):
            slot = (row // pair_rows) * slots_each + row % pair_rows
            for block in range(blocks):
                zsend_back[row, here, lanes_of(block)] = gather_f32[
                    block, pl.ds(slot + pair_rows, chunk_span, stride=row_slots), :
                ].astype(jnp.bfloat16)
        zb_copy(chunk).start()
        for row in range(row_count):
            slot = (row // pair_rows) * slots_each + row % pair_rows
            for block in range(blocks):
                yown[row, here, lanes_of(block)] = gather_f32[
                    block, pl.ds(slot, chunk_span, stride=row_slots), :
                ].astype(jnp.bfloat16)

    spectral_chunk(0)
    for chunk in range(1, chunk_count):
        spectral_chunk(chunk)
        return_chunk(chunk - 1)
    return_chunk(chunk_count - 1)
    for chunk in range(chunk_count):
        zb_copy(chunk).wait_recv()

    def finish(row, carry):
        spatial = dot_nn(analysis_ref[half], yown[row]) + dot_nn(
            analysis_ref[1 - half], zrecv_back[row]
        )
        out_ref[row] = (
            cot_ref[row].astype(jnp.float32) + spatial * (1.0 / lon_count)
        ).astype(jnp.bfloat16)
        return carry

    lax.fori_loop(0, row_count, finish, 0)

    def drain_rows(row, carry):
        for step in range(1, member_count):
            point_copy(row, step).wait_send()
            cot_copy(row, step).wait_send()
        z_copy(row).wait_send()
        return carry

    lax.fori_loop(0, row_count, drain_rows, 0)

    def drain_plane(step, carry):
        for pair in range(pair_count):
            p_copy(pair, step).wait_send()
        for chunk in range(chunk_count):
            r_copy(chunk, step).wait_send()
        return carry

    lax.fori_loop(1, plane_count, drain_plane, 0)
    for chunk in range(chunk_count):
        zb_copy(chunk).wait_send()


def shards(
    grid_input, saved_mixed, target, land_weight, mix_weight, degree_gain, up_weight, down_weight
):
    row_count, lon_count, channels = grid_input.shape[1:]
    hidden = up_weight.shape[1]
    total_lat = degree_gain.shape[0]
    member_count = lax.axis_size("member")
    plane_count = lax.axis_size("lat") // 2
    part = lon_count // member_count
    mode_count = lon_count // 2
    orders_each = mode_count // (2 * plane_count)
    pair_count = row_count // pair_rows
    chunk_count = orders_each // 2
    half_rows = mode_count
    piece = 2 * pair_rows * 2 * orders_each
    member = lax.axis_index("member")
    lat = lax.axis_index("lat")
    half = lat // plane_count
    spot = lat % plane_count

    local_angles = ((lat * row_count + jnp.arange(row_count)).astype(jnp.float32) + 0.5) * (
        math.pi / total_lat
    )
    own_land = lax.dynamic_slice_in_dim(land_weight, member * part, part, 1)
    weights = (jnp.sin(local_angles)[:, None] * own_land.astype(jnp.float32))[:, :, None]

    pair_index = jnp.arange(pair_count)[:, None, None, None]
    side = jnp.arange(2)[None, :, None, None]
    inner = jnp.arange(pair_rows)[None, None, :, None]
    sender = jnp.arange(plane_count)[None, None, None, :]
    side_half = jnp.where(side == 0, half, 1 - half)
    lat_rows = (
        (side_half * plane_count + sender) * row_count + pair_index * pair_rows + inner
    ).reshape(-1)
    angles = (lat_rows.astype(jnp.float32) + 0.5) * (math.pi / total_lat)
    quad_weight = jnp.sin(angles) * (math.pi / total_lat)
    orders = half * (mode_count // 2) + spot * orders_each + jnp.arange(orders_each)
    start_log, order_f, cosine = legendre_start(orders, angles, total_lat)
    synth, analysis = fourier_tables(lon_count, plane_count, orders_each)

    blocks = max(channels // 128, 1)
    bf16 = jnp.bfloat16
    f32 = jnp.float32
    vmem = pl.BlockSpec(memory_space=pltpu.VMEM)
    anywhere = pl.BlockSpec(memory_space=pl.ANY)
    dma = pltpu.SemaphoreType.DMA
    result = pl.pallas_call(
        fused_kernel,
        out_shape=jax.ShapeDtypeStruct((row_count, lon_count, channels), bf16),
        in_specs=[vmem, vmem, anywhere] + [vmem] * 11,
        out_specs=vmem,
        scratch_shapes=[
            pltpu.VMEM((row_count, part, channels), bf16),
            pltpu.VMEM((member_count - 1, row_count, part, channels), bf16),
            pltpu.VMEM((member_count, row_count, part, channels), bf16),
            pltpu.VMEM((member_count - 1, row_count, part, channels), bf16),
            pltpu.VMEM((row_count, lon_count, channels), bf16),
            pltpu.VMEM((row_count, lon_count, hidden), bf16),
            pltpu.VMEM((lon_count, channels), bf16),
            pltpu.VMEM((blocks, plane_count * piece, channels // blocks), f32),
            pltpu.VMEM((row_count, half_rows, channels), bf16),
            pltpu.VMEM((row_count, half_rows, channels), bf16),
            pltpu.VMEM((pair_count, plane_count, piece, channels), bf16),
            pltpu.VMEM((plane_count, pair_count, piece, channels), bf16),
            pltpu.VMEM((blocks, plane_count * pair_count * piece, channels // blocks), f32),
            pltpu.VMEM((total_lat,) + start_log.shape, f32),
            pltpu.VMEM((orders_each, total_lat, total_lat), bf16),
            pltpu.VMEM((total_lat, 2 * channels), bf16),
            pltpu.VMEM((chunk_count, plane_count, piece, channels), bf16),
            pltpu.VMEM((chunk_count, plane_count, piece, channels), bf16),
            pltpu.VMEM((row_count, half_rows, channels), bf16),
            pltpu.VMEM((row_count, half_rows, channels), bf16),
            pltpu.VMEM((row_count, half_rows, channels), bf16),
            dma,
            dma((row_count, member_count - 1)),
            dma((row_count, member_count - 1)),
            dma((row_count, member_count - 1)),
            dma((row_count, member_count - 1)),
            dma((row_count,)),
            dma((row_count,)),
            dma((pair_count, plane_count)),
            dma((pair_count, plane_count)),
            dma((chunk_count, plane_count)),
            dma((chunk_count, plane_count)),
            dma((chunk_count,)),
            dma((chunk_count,)),
        ],
        compiler_params=pltpu.CompilerParams(
            collective_id=0, has_side_effects=True, vmem_limit_bytes=62 * 2**20
        ),
    )(
        grid_input[0],
        saved_mixed[0],
        target,
        weights,
        mix_weight,
        degree_gain[:, None],
        up_weight,
        down_weight,
        synth,
        analysis,
        start_log,
        order_f,
        cosine,
        quad_weight[:, None],
    )
    return result[None]


def solution(mesh):
    in_specs = (
        P("member", "lat", None, None),
        P("member", "lat", None, None),
        P("lat", None, None),
        P("lat", None),
        P(),
        P(),
        P(),
        P(),
    )
    out_specs = P("member", "lat", None, None)
    return jax.shard_map(shards, mesh=mesh, in_specs=in_specs, out_specs=out_specs, check_vma=False)
```

```python
import functools
import math

import jax
import jax.numpy as jnp
import ml_dtypes
import numpy as np
from jax import lax
from jax.experimental import pallas as pl
from jax.experimental.pallas import tpu as pltpu
from jax.sharding import PartitionSpec as P

kappa_gelu = 0.7978845608
cubic_gelu = 0.044715
smooth_square = 0.25
pair_rows = 2
low_each = 4
high_each = 4
low_chunks = 2
MESH = pl.DeviceIdType.MESH


def gelu_parts(inputs):
    squared = inputs * inputs
    tanh_part = jnp.tanh(kappa_gelu * inputs * (1.0 + cubic_gelu * squared))
    half_sum = 0.5 * (1.0 + tanh_part)
    values = inputs * half_sum
    slopes = half_sum + 0.5 * inputs * (1.0 - tanh_part * tanh_part) * (
        kappa_gelu + (3.0 * cubic_gelu * kappa_gelu) * squared
    )
    return (values, slopes)


def slope_abs(difference):
    return difference * lax.rsqrt(difference * difference + smooth_square)


def dot_nn(lhs, rhs):
    return lax.dot_general(lhs, rhs, (((1,), (0,)), ((), ())), preferred_element_type=jnp.float32)


def dot_nt(lhs, rhs):
    return lax.dot_general(lhs, rhs, (((1,), (1,)), ((), ())), preferred_element_type=jnp.float32)


def dot_tn(lhs, rhs):
    return lax.dot_general(lhs, rhs, (((0,), (0,)), ((), ())), preferred_element_type=jnp.float32)


def orders_low(plane_count):
    return np.arange(2 * plane_count * low_each).reshape(2, plane_count, low_each)


def orders_high(plane_count):
    first = 2 * plane_count * low_each
    return first + np.arange(high_each)[None, :] * plane_count + np.arange(plane_count)[:, None]


def fourier_tables(lon_count, plane_count):
    positions = np.arange(lon_count)

    def entries(orders):
        phase = (orders[..., None] * positions) % lon_count
        angles = phase.astype(np.float32) * np.float32(2.0 * math.pi / lon_count)
        factor = np.where(orders == 0, 1.0, 2.0).astype(np.float32)[..., None]
        plain = np.stack([np.cos(angles), -np.sin(angles)], axis=-2)
        return (plain * factor[..., None], plain)

    low = orders_low(plane_count)
    high = orders_high(plane_count)
    rows = plane_count * low_each * 2
    low_synth, low_plain = entries(low)
    high_synth, high_plain = entries(high)
    synth = np.concatenate(
        [low_synth.reshape(2, rows, lon_count), high_synth.reshape(1, rows, lon_count)]
    )
    low_plain = low_plain.reshape(2, plane_count, low_chunks, -1, lon_count)
    low_plain = low_plain.transpose(0, 2, 1, 3, 4).reshape(2, rows, lon_count)
    analysis = np.concatenate([low_plain, high_plain.reshape(1, rows, lon_count)])
    analysis = analysis.transpose(0, 2, 1)
    return (
        jnp.asarray(synth.astype(ml_dtypes.bfloat16)),
        jnp.asarray(analysis.astype(ml_dtypes.bfloat16)),
    )


def latitude_tables(row_count, plane_count, total_lat):
    half = np.arange(2)[:, None, None, None]
    side = np.arange(2)[None, :, None, None]
    row = np.arange(row_count)[None, None, :, None]
    sender = np.arange(plane_count)[None, None, None, :]
    side_half = np.where(side == 0, half, 1 - half)
    lat_rows = ((side_half * plane_count + sender) * row_count + row).reshape(2, total_lat)
    angles = (lat_rows + 0.5) * (math.pi / total_lat)
    low = orders_low(plane_count)
    high = np.broadcast_to(orders_high(plane_count)[None], (2, plane_count, high_each))
    orders = np.concatenate([low, high], axis=2)
    factor_index = np.arange(1, total_lat + 1)
    ratios = np.log((2.0 * factor_index - 1.0) / (2.0 * factor_index))
    partial_log = np.concatenate([[0.0], np.cumsum(ratios)])[orders]
    start_log = (0.5 * np.log(orders + 0.5) + 0.5 * partial_log)[..., None] + orders[
        ..., None
    ] * np.log(np.sin(angles))[:, None, None, :]
    start_log = start_log.reshape(2 * plane_count, low_each + high_each, total_lat)
    cosine = np.broadcast_to(np.cos(angles)[:, None, :], (2, low_each + high_each, total_lat))
    quad = np.sin(angles) * (math.pi / total_lat)
    quad = np.broadcast_to(quad[:, :, None], (2, total_lat, 128))
    local = (np.arange(total_lat).reshape(2 * plane_count, row_count) + 0.5) * (math.pi / total_lat)
    area = np.zeros((2 * plane_count, 8, 128))
    area[:, :row_count, :] = np.sin(local)[:, :, None]
    return tuple(jnp.asarray(table.astype(np.float32)) for table in (start_log, cosine, quad, area))


def legendre_fill(block, start_ref, order_f, cosine_ref, rows_ref, table_ref, high_ref):
    degree_count = rows_ref.shape[0]
    cosine = cosine_ref[...]
    zeros = jnp.zeros(cosine.shape, jnp.float32)

    def advance_block(step, state):
        older, newer, log_scale = state
        half_scale = jnp.exp(0.5 * log_scale)
        for offset in range(block):
            degree = step * block + offset
            degree_f = degree.astype(jnp.float32)
            below = degree_f - 1.0
            alpha_rec = jnp.sqrt(
                jnp.maximum(4.0 * degree_f * degree_f - 1.0, 1.0)
                / jnp.maximum(degree_f * degree_f - order_f * order_f, 1.0)
            )
            beta_rec = jnp.sqrt(
                jnp.maximum(below * below - order_f * order_f, 0.0)
                / jnp.maximum(4.0 * below * below - 1.0, 1.0)
            )
            recurred = alpha_rec * (cosine * newer - beta_rec * older)
            fresh = jnp.where(
                degree_f < order_f, 0.0, jnp.where(degree_f == order_f, 1.0, recurred)
            )
            rows_ref[degree] = (fresh * half_scale) * half_scale
            older, newer = newer, fresh
        largest = jnp.maximum(jnp.abs(older), jnp.abs(newer))
        norm_value = jnp.where(largest > 0.0, largest, 1.0)
        return (older / norm_value, newer / norm_value, log_scale + jnp.log(norm_value))

    lax.fori_loop(0, degree_count // block, advance_block, (zeros, zeros, start_ref[...]))
    for slot in range(low_each):
        table_ref[slot] = rows_ref[:, slot, :].astype(jnp.bfloat16)
    for slot in range(high_each):
        kept = rows_ref[degree_count - high_ref.shape[1] :, low_each + slot, :]
        high_ref[slot] = kept[:, : high_ref.shape[2]].astype(jnp.bfloat16)


def fused_kernel(
    grid_ref, saved_ref, target_ref, land_ref, mix_ref, gain_ref, up_ref, down_ref,
    synth_ref, analysis_ref, start_all, cosine_all, quad_all, area_all,
    out_ref,
    own_target, start_ref, cosine_ref, quad_ref, area_ref, weight_rows, weight_ref, gain_low,
    gain_high,
    send_points, recv_points, send_cot, cot_ref, slopes_ref, mixed_ref,
    gather_f32, gather_high, zsend, zrecv, psend, precv, wave_f32, rows_ref, table_ref, high_ref,
    wave_ref, high_f32, high_send, high_recv, high_coeff, total_ref,
    rsend, rrecv, yown, yhigh, zsend_back, zrecv_back,
    local_sem, point_ss, point_rs, cot_ss, cot_rs, z_ss, z_rs, p_ss, p_rs, r_ss, r_rs,
    zb_ss, zb_rs, h_ss, h_rs,
):
    row_count, lon_count, channels = saved_ref.shape
    member_count = recv_points.shape[0]
    part = lon_count // member_count
    plane_count = precv.shape[0]
    pair_count = precv.shape[1]
    piece = precv.shape[2]
    chunk_count = rrecv.shape[0]
    chunk_orders = low_each // low_chunks
    chunk_span = plane_count * 2 * chunk_orders
    row_slots = 2 * row_count
    own_lats = row_count * plane_count
    total_lat = 2 * own_lats
    low_piece = 2 * low_each * 2 * pair_rows
    region = (high_each + 1) * plane_count

    member = lax.axis_index("member")
    lat = lax.axis_index("lat")
    half = lat // plane_count
    spot = lat - half * plane_count
    partner = {"lat": lax.rem(lat + plane_count, 2 * plane_count)}

    def member_peer(step):
        return {"member": lax.rem(member + step, member_count)}

    def plane_spot(step):
        return lax.rem(spot + step, plane_count)

    def plane_peer(step):
        return {"lat": half * plane_count + plane_spot(step)}

    local_copies = [
        pltpu.make_async_copy(
            target_ref.at[:, pl.ds(member * part, part), :], own_target, local_sem.at[0]
        ),
        pltpu.make_async_copy(start_all.at[lat], start_ref, local_sem.at[1]),
        pltpu.make_async_copy(cosine_all.at[half], cosine_ref, local_sem.at[2]),
        pltpu.make_async_copy(quad_all.at[half], quad_ref, local_sem.at[3]),
        pltpu.make_async_copy(area_all.at[lat], area_ref, local_sem.at[4]),
    ]
    for copy in local_copies:
        copy.start()

    barrier = pltpu.get_barrier_semaphore()
    for step in range(1, member_count):
        pl.semaphore_signal(barrier, inc=1, device_id=member_peer(step), device_id_type=MESH)
    pl.semaphore_signal(barrier, inc=1, device_id=partner, device_id_type=MESH)

    def greet(step, carry):
        pl.semaphore_signal(barrier, inc=1, device_id=plane_peer(step), device_id_type=MESH)
        return carry

    lax.fori_loop(1, plane_count, greet, 0)
    pl.semaphore_wait(barrier, member_count - 1 + 1 + plane_count - 1)

    def point_copy(row, step):
        return pltpu.make_async_remote_copy(
            src_ref=send_points.at[step - 1, row],
            dst_ref=recv_points.at[member_count - step, row],
            send_sem=point_ss.at[row, step - 1],
            recv_sem=point_rs.at[row, step - 1],
            device_id=member_peer(step),
            device_id_type=MESH,
        )

    def cot_copy(row, step):
        return pltpu.make_async_remote_copy(
            src_ref=send_cot.at[step - 1, row],
            dst_ref=cot_ref.at[row, pl.ds(member * part, part), :],
            send_sem=cot_ss.at[row, step - 1],
            recv_sem=cot_rs.at[row, step - 1],
            device_id=member_peer(step),
            device_id_type=MESH,
        )

    def z_copy(row):
        return pltpu.make_async_remote_copy(
            src_ref=zsend.at[row],
            dst_ref=zrecv.at[row],
            send_sem=z_ss.at[row],
            recv_sem=z_rs.at[row],
            device_id=partner,
            device_id_type=MESH,
        )

    def p_copy(pair, step):
        return pltpu.make_async_remote_copy(
            src_ref=psend.at[pair, plane_spot(step)],
            dst_ref=precv.at[spot, pair],
            send_sem=p_ss.at[pair, step],
            recv_sem=p_rs.at[pair, step],
            device_id=plane_peer(step),
            device_id_type=MESH,
        )

    def r_copy(chunk, step):
        return pltpu.make_async_remote_copy(
            src_ref=rsend.at[chunk, plane_spot(step)],
            dst_ref=rrecv.at[chunk, spot],
            send_sem=r_ss.at[chunk, step],
            recv_sem=r_rs.at[chunk, step],
            device_id=plane_peer(step),
            device_id_type=MESH,
        )

    def zb_copy(chunk):
        return pltpu.make_async_remote_copy(
            src_ref=zsend_back.at[:, pl.ds(chunk * chunk_span, chunk_span), :],
            dst_ref=zrecv_back.at[:, pl.ds(chunk * chunk_span, chunk_span), :],
            send_sem=zb_ss.at[chunk],
            recv_sem=zb_rs.at[chunk],
            device_id=partner,
            device_id_type=MESH,
        )

    def forward_part(row, step):
        begin = pl.multiple_of(lax.rem(member + step, member_count) * part, part)
        hidden_pre = dot_nn(saved_ref[row, pl.ds(begin, part), :], up_ref[...])
        values, slopes = gelu_parts(hidden_pre)
        slopes_ref[row, pl.ds(begin, part), :] = slopes.astype(jnp.bfloat16)
        branch = dot_nn(values.astype(jnp.bfloat16), down_ref[...])
        summed = grid_ref[row, pl.ds(begin, part), :].astype(jnp.float32) + branch
        return summed.astype(jnp.bfloat16)

    def forward_row(row):
        def one(step, carry):
            send_points[step - 1, row] = forward_part(row, step)
            point_copy(row, step).start()
            return carry

        lax.fori_loop(1, member_count, one, 0)
        recv_points[0, row] = forward_part(row, 0)

    def high_copy():
        theirs = pl.ds(pl.multiple_of((1 - half) * region, region), region)
        return pltpu.make_async_remote_copy(
            src_ref=high_send.at[theirs, :],
            dst_ref=high_recv,
            send_sem=h_ss.at[0],
            recv_sem=h_rs.at[0],
            device_id=partner,
            device_id_type=MESH,
        )

    def coeff_copy():
        mine = pl.ds(pl.multiple_of(half * region, region), region)
        return pltpu.make_async_remote_copy(
            src_ref=high_coeff.at[mine, :],
            dst_ref=high_coeff.at[mine, :],
            send_sem=h_ss.at[1],
            recv_sem=h_rs.at[1],
            device_id=partner,
            device_id_type=MESH,
        )

    strip = 16 if part % 16 == 0 else part

    def loss_row(row):
        for step in range(1, member_count):
            point_copy(row, step).wait_recv()
        own_begin = pl.multiple_of(member * part, part)

        def one(index, carry):
            begin = pl.multiple_of(index * strip, strip)
            here = pl.ds(begin, strip)
            values = [
                recv_points[slot, row, here, :].astype(jnp.float32) for slot in range(member_count)
            ]
            totals = [jnp.zeros(values[0].shape, jnp.float32) for slot in range(member_count)]
            for first in range(member_count):
                for second in range(first + 1, member_count):
                    slope = slope_abs(values[first] - values[second])
                    totals[first] = totals[first] + slope
                    totals[second] = totals[second] - slope
            wanted = own_target[row, here, :].astype(jnp.float32)
            spot_here = pl.ds(pl.multiple_of(own_begin + begin, strip), strip)
            weights = weight_ref[spot_here, row : row + 1]
            for slot in range(member_count):
                term = weights * (
                    slope_abs(values[slot] - wanted) / member_count
                    - totals[slot] / (member_count * member_count)
                )
                if slot == 0:
                    cot_ref[row, spot_here, :] = term.astype(jnp.bfloat16)
                else:
                    send_cot[slot - 1, row, here, :] = term.astype(jnp.bfloat16)
            return carry

        lax.fori_loop(0, part // strip, one, 0)
        for step in range(1, member_count):
            cot_copy(row, step).start()

    blocks, lane_width = gather_f32.shape[0], gather_f32.shape[2]

    def lanes_of(block):
        return slice(block * lane_width, (block + 1) * lane_width)

    def scatter_rows(target, first, count, stride, values):
        for block in range(blocks):
            target[block, pl.ds(first, count, stride=stride), :] = values[:, lanes_of(block)]

    def backward_row(row, own_slot):
        for step in range(1, member_count):
            cot_copy(row, step).wait_recv()

        def one(index, carry):
            here = pl.ds(pl.multiple_of(index * part, part), part)
            act_grad = dot_nt(cot_ref[row, here, :], down_ref[...])
            pre_grad = (act_grad * slopes_ref[row, here, :].astype(jnp.float32)).astype(jnp.bfloat16)
            mixed_ref[here, :] = dot_nt(pre_grad, up_ref[...]).astype(jnp.bfloat16)
            return carry

        lax.fori_loop(0, member_count, one, 0)
        other = dot_nn(synth_ref[1 - half], mixed_ref[...])
        zsend[row] = other.astype(jnp.bfloat16)
        z_copy(row).start()
        own = dot_nn(synth_ref[half], mixed_ref[...])
        scatter_rows(gather_f32, own_slot, own.shape[0], 2 * pair_rows, own)
        high = dot_nn(synth_ref[2], mixed_ref[...])
        scatter_rows(gather_high, own_slot, high.shape[0], pair_rows, high)

    def plane_pair(pair):
        for inner in range(pair_rows):
            row = pair * pair_rows + inner
            z_copy(row).wait_recv()
            scatter_rows(
                gather_f32,
                pair_rows + inner,
                zrecv.shape[1],
                2 * pair_rows,
                zrecv[row].astype(jnp.float32),
            )
        for block in range(blocks):
            psend[pair, :, :low_piece, lanes_of(block)] = (
                gather_f32[block, : plane_count * low_piece]
                .reshape(plane_count, low_piece, lane_width)
                .astype(jnp.bfloat16)
            )
            psend[pair, :, low_piece:, lanes_of(block)] = (
                gather_high[block]
                .reshape(plane_count, piece - low_piece, lane_width)
                .astype(jnp.bfloat16)
            )

        def one(step, carry):
            p_copy(pair, step).start()
            return carry

        lax.fori_loop(1, plane_count, one, 0)
        precv[spot, pair] = psend[pair, spot]

    group = pair_count * piece

    def await_pair(pair):
        def one(step, carry):
            p_copy(pair, step).wait_recv()
            return carry

        lax.fori_loop(1, plane_count, one, 0)

        def widen(index, carry):
            here = pl.ds(pl.multiple_of(index * group + pair * piece, piece), piece)
            for block in range(blocks):
                wave_f32[block, here, :] = precv[index, pair, :, lanes_of(block)].astype(
                    jnp.float32
                )
            return carry

        lax.fori_loop(0, plane_count, widen, 0)

    def collect(first, begin, phase):
        for block in range(blocks):
            lane_begin = phase * channels + block * lane_width
            wave_ref[begin : begin + plane_count, lane_begin : lane_begin + lane_width] = wave_f32[
                block, pl.ds(first, plane_count, stride=group), :
            ].astype(jnp.bfloat16)

    def mix(gained):
        return jnp.concatenate(
            [
                dot_nt(gained[:, :channels], mix_ref[...]).astype(jnp.bfloat16),
                dot_nt(gained[:, channels:], mix_ref[...]).astype(jnp.bfloat16),
            ],
            axis=1,
        )

    def send_chunk(chunk):
        for block in range(blocks):
            rsend[chunk, :, :, lanes_of(block)] = (
                gather_f32[block].reshape(plane_count, piece, lane_width).astype(jnp.bfloat16)
            )

        def one(step, carry):
            r_copy(chunk, step).start()
            return carry

        lax.fori_loop(1, plane_count, one, 0)
        rrecv[chunk, spot] = rsend[chunk, spot]

    def receive_chunk(chunk):
        def one(step, carry):
            r_copy(chunk, step).wait_recv()
            return carry

        lax.fori_loop(1, plane_count, one, 0)
        for block in range(blocks):
            gather_f32[block] = (
                rrecv[chunk, :, :, lanes_of(block)]
                .reshape(plane_count * piece, lane_width)
                .astype(jnp.float32)
            )

    def low_chunk(chunk):
        def one_order(inner, carry):
            order = chunk * chunk_orders + inner
            for phase in range(2):
                key = order * 2 + phase
                for side in range(2):
                    for row in range(row_count):
                        slot = side * pair_rows + row % pair_rows
                        first = (row // pair_rows) * piece + key * 2 * pair_rows + slot
                        collect(first, (side * row_count + row) * plane_count, phase)
            degree_grad = dot_nn(table_ref[order], wave_ref[...])
            coeff_grad = mix((degree_grad * gain_low[:, 0:1]).astype(jnp.bfloat16))
            lat_grad = dot_tn(table_ref[order], coeff_grad) * quad_ref[:, 0:1]
            for phase in range(2):
                for slot in range(row_slots):
                    scatter_rows(
                        gather_f32,
                        (inner * 2 + phase) * row_slots + slot,
                        plane_count,
                        piece,
                        lat_grad[
                            slot * plane_count : (slot + 1) * plane_count,
                            phase * channels : (phase + 1) * channels,
                        ],
                    )
            return carry

        lax.fori_loop(0, chunk_orders, one_order, 0)
        send_chunk(chunk)

    high_first = [0, 5 * plane_count, 8 * plane_count, 4 * plane_count]
    high_size = [(high_each - slot) * plane_count for slot in range(high_each)]

    def high_analysis():
        for slot in range(high_each):
            for phase in range(2):
                key = slot * 2 + phase
                for row in range(row_count):
                    first = (
                        (row // pair_rows) * piece
                        + low_piece
                        + key * pair_rows
                        + row % pair_rows
                    )
                    collect(first, row * plane_count, phase)
            here = slice(high_first[slot], high_first[slot] + high_size[slot])
            total = dot_nn(high_ref[slot, slot * plane_count :, :], wave_ref[:own_lats, :])
            high_f32[here, :] = total
            high_send[here, :] = total.astype(jnp.bfloat16)
        high_copy().start()

    def high_middle():
        high_copy().wait_recv()
        mine = pl.ds(pl.multiple_of(half * region, region), region)
        total = high_f32[mine, :] + high_recv[...].astype(jnp.float32)
        gained = (total * gain_high[mine, 0:1]).astype(jnp.bfloat16)
        high_coeff[mine, :] = mix(gained)
        coeff_copy().start()

    def high_synthesis():
        coeff_copy().wait_recv()
        for slot in range(high_each):
            here = slice(high_first[slot], high_first[slot] + high_size[slot])
            lat_grad = (
                dot_tn(high_ref[slot, slot * plane_count :, :], high_coeff[here, :])
                * quad_ref[:own_lats, 0:1]
            )
            for phase in range(2):
                for row in range(row_count):
                    scatter_rows(
                        gather_f32,
                        (slot * 2 + phase) * row_count + row,
                        plane_count,
                        piece,
                        lat_grad[
                            row * plane_count : (row + 1) * plane_count,
                            phase * channels : (phase + 1) * channels,
                        ],
                    )
        send_chunk(low_chunks)

    def return_low(chunk):
        receive_chunk(chunk)
        here = pl.ds(chunk * chunk_span, chunk_span)
        for row in range(row_count):
            for block in range(blocks):
                zsend_back[row, here, lanes_of(block)] = gather_f32[
                    block, pl.ds(row_count + row, chunk_span, stride=row_slots), :
                ].astype(jnp.bfloat16)
        zb_copy(chunk).start()
        for row in range(row_count):
            for block in range(blocks):
                yown[row, here, lanes_of(block)] = gather_f32[
                    block, pl.ds(row, chunk_span, stride=row_slots), :
                ].astype(jnp.bfloat16)

    def return_high():
        receive_chunk(low_chunks)
        for row in range(row_count):
            for block in range(blocks):
                yhigh[row, :, lanes_of(block)] = gather_f32[
                    block, pl.ds(row, yhigh.shape[1], stride=row_count), :
                ].astype(jnp.bfloat16)

    forward_row(0)
    forward_row(1)
    for copy in local_copies:
        copy.wait()
    spread = lax.broadcasted_iota(jnp.int32, cosine_ref.shape, 0)
    low_order = half * (plane_count * low_each) + spot * low_each + spread
    high_order = 2 * plane_count * low_each + (spread - low_each) * plane_count + spot
    order_f = jnp.where(spread < low_each, low_order, high_order).astype(jnp.float32)
    weight_rows[...] = jnp.zeros(weight_rows.shape, jnp.float32)
    weight_rows[:row_count, :] = land_ref[...].astype(jnp.float32) * area_ref[:row_count, 0:1]
    weight_ref[...] = weight_rows[...].T
    gain_low[...] = jnp.broadcast_to(gain_ref[...], (8, total_lat)).T
    for slot in range(high_each):
        gain_high[high_first[slot] : high_first[slot] + high_size[slot], :] = gain_low[
            total_lat - high_size[slot] :, :
        ]
    legendre_fill(
        math.gcd(total_lat, 16), start_ref, order_f, cosine_ref, rows_ref, table_ref, high_ref
    )
    for row in range(row_count):
        loss_row(row)
        if row + 2 < row_count:
            forward_row(row + 2)
        if row >= 1:
            backward_row(row - 1, (row - 1) % pair_rows)
            if row % pair_rows == 0:
                plane_pair(row // pair_rows - 1)
    backward_row(row_count - 1, (row_count - 1) % pair_rows)
    for pair in range(pair_count - 1):
        await_pair(pair)
    plane_pair(pair_count - 1)
    await_pair(pair_count - 1)

    high_analysis()
    low_chunk(0)
    high_middle()
    for chunk in range(1, low_chunks):
        low_chunk(chunk)
        return_low(chunk - 1)
    high_synthesis()
    return_low(low_chunks - 1)
    return_high()

    def own_part(row, carry):
        total_ref[row] = dot_nn(analysis_ref[half], yown[row]) + dot_nn(analysis_ref[2], yhigh[row])
        return carry

    lax.fori_loop(0, row_count, own_part, 0)
    for chunk in range(low_chunks):
        zb_copy(chunk).wait_recv()

    def finish(row, carry):
        spatial = total_ref[row] + dot_nn(analysis_ref[1 - half], zrecv_back[row])
        out_ref[row] = (
            cot_ref[row].astype(jnp.float32) + spatial * (1.0 / lon_count)
        ).astype(jnp.bfloat16)
        return carry

    lax.fori_loop(0, row_count, finish, 0)

    def drain_rows(row, carry):
        for step in range(1, member_count):
            point_copy(row, step).wait_send()
            cot_copy(row, step).wait_send()
        z_copy(row).wait_send()
        return carry

    lax.fori_loop(0, row_count, drain_rows, 0)

    def drain_plane(step, carry):
        for pair in range(pair_count):
            p_copy(pair, step).wait_send()
        for chunk in range(chunk_count):
            r_copy(chunk, step).wait_send()
        return carry

    lax.fori_loop(1, plane_count, drain_plane, 0)
    for chunk in range(low_chunks):
        zb_copy(chunk).wait_send()
    high_copy().wait_send()
    coeff_copy().wait_send()


def shards(
    grid_input, saved_mixed, target, land_weight, mix_weight, degree_gain, up_weight, down_weight
):
    row_count, lon_count, channels = grid_input.shape[1:]
    hidden = up_weight.shape[1]
    total_lat = degree_gain.shape[0]
    member_count = lax.axis_size("member")
    plane_count = lax.axis_size("lat") // 2
    part = lon_count // member_count
    pair_count = row_count // pair_rows
    chunk_count = low_chunks + 1
    keys = plane_count * 2 * low_each
    low_piece = 2 * low_each * 2 * pair_rows
    piece = low_piece + 2 * high_each * pair_rows
    order_slots = low_each + high_each
    region = (high_each + 1) * plane_count
    own_lats = row_count * plane_count
    synth, analysis = fourier_tables(lon_count, plane_count)
    start_log, cosine, quad, area = latitude_tables(row_count, plane_count, total_lat)

    blocks = max(channels // 128, 1)
    bf16 = jnp.bfloat16
    f32 = jnp.float32
    vmem = pl.BlockSpec(memory_space=pltpu.VMEM)
    anywhere = pl.BlockSpec(memory_space=pl.ANY)
    dma = pltpu.SemaphoreType.DMA
    result = pl.pallas_call(
        fused_kernel,
        out_shape=jax.ShapeDtypeStruct((row_count, lon_count, channels), bf16),
        in_specs=[vmem, vmem, anywhere] + [vmem] * 7 + [anywhere] * 4,
        out_specs=vmem,
        scratch_shapes=[
            pltpu.VMEM((row_count, part, channels), bf16),
            pltpu.VMEM((order_slots, total_lat), f32),
            pltpu.VMEM((order_slots, total_lat), f32),
            pltpu.VMEM((total_lat, 128), f32),
            pltpu.VMEM((8, 128), f32),
            pltpu.VMEM((8, lon_count), f32),
            pltpu.VMEM((lon_count, 8), f32),
            pltpu.VMEM((total_lat, 8), f32),
            pltpu.VMEM((2 * region, 8), f32),
            pltpu.VMEM((member_count - 1, row_count, part, channels), bf16),
            pltpu.VMEM((member_count, row_count, part, channels), bf16),
            pltpu.VMEM((member_count - 1, row_count, part, channels), bf16),
            pltpu.VMEM((row_count, lon_count, channels), bf16),
            pltpu.VMEM((row_count, lon_count, hidden), bf16),
            pltpu.VMEM((lon_count, channels), bf16),
            pltpu.VMEM((blocks, plane_count * piece, channels // blocks), f32),
            pltpu.VMEM((blocks, plane_count * (piece - low_piece), channels // blocks), f32),
            pltpu.VMEM((row_count, keys, channels), bf16),
            pltpu.VMEM((row_count, keys, channels), bf16),
            pltpu.VMEM((pair_count, plane_count, piece, channels), bf16),
            pltpu.VMEM((plane_count, pair_count, piece, channels), bf16),
            pltpu.VMEM((blocks, plane_count * pair_count * piece, channels // blocks), f32),
            pltpu.VMEM((total_lat, order_slots, total_lat), f32),
            pltpu.VMEM((low_each, total_lat, total_lat), bf16),
            pltpu.VMEM((high_each, high_each * plane_count, own_lats), bf16),
            pltpu.VMEM((total_lat, 2 * channels), bf16),
            pltpu.VMEM((2 * region, 2 * channels), f32),
            pltpu.VMEM((2 * region, 2 * channels), bf16),
            pltpu.VMEM((region, 2 * channels), bf16),
            pltpu.VMEM((2 * region, 2 * channels), bf16),
            pltpu.VMEM((row_count, lon_count, channels), f32),
            pltpu.VMEM((chunk_count, plane_count, piece, channels), bf16),
            pltpu.VMEM((chunk_count, plane_count, piece, channels), bf16),
            pltpu.VMEM((row_count, keys, channels), bf16),
            pltpu.VMEM((row_count, keys, channels), bf16),
            pltpu.VMEM((row_count, keys, channels), bf16),
            pltpu.VMEM((row_count, keys, channels), bf16),
            dma((5,)),
            dma((row_count, member_count - 1)),
            dma((row_count, member_count - 1)),
            dma((row_count, member_count - 1)),
            dma((row_count, member_count - 1)),
            dma((row_count,)),
            dma((row_count,)),
            dma((pair_count, plane_count)),
            dma((pair_count, plane_count)),
            dma((chunk_count, plane_count)),
            dma((chunk_count, plane_count)),
            dma((low_chunks,)),
            dma((low_chunks,)),
            dma((2,)),
            dma((2,)),
        ],
        compiler_params=pltpu.CompilerParams(
            collective_id=0, has_side_effects=True, vmem_limit_bytes=63 * 2**20
        ),
    )(
        grid_input[0],
        saved_mixed[0],
        target,
        land_weight,
        mix_weight,
        degree_gain[None, :],
        up_weight,
        down_weight,
        synth,
        analysis,
        start_log,
        cosine,
        quad,
        area,
    )
    return result[None]


def solution(mesh):
    in_specs = (
        P("member", "lat", None, None),
        P("member", "lat", None, None),
        P("lat", None, None),
        P("lat", None),
        P(),
        P(),
        P(),
        P(),
    )
    out_specs = P("member", "lat", None, None)
    return jax.shard_map(shards, mesh=mesh, in_specs=in_specs, out_specs=out_specs, check_vma=False)
```

```python
import functools
import math

import jax
import jax.numpy as jnp
import ml_dtypes
import numpy as np
from jax import lax
from jax.experimental import pallas as pl
from jax.experimental.pallas import tpu as pltpu
from jax.sharding import PartitionSpec as P

kappa_gelu = 0.7978845608
cubic_gelu = 0.044715
smooth_square = 0.25
pair_rows = 2
low_each = 4
high_each = 4
MESH = pl.DeviceIdType.MESH


def gelu_parts(inputs):
    squared = inputs * inputs
    tanh_part = jnp.tanh(kappa_gelu * inputs * (1.0 + cubic_gelu * squared))
    half_sum = 0.5 * (1.0 + tanh_part)
    values = inputs * half_sum
    slopes = half_sum + 0.5 * inputs * (1.0 - tanh_part * tanh_part) * (
        kappa_gelu + (3.0 * cubic_gelu * kappa_gelu) * squared
    )
    return (values, slopes)


def slope_abs(difference):
    return difference * lax.rsqrt(difference * difference + smooth_square)


def dot_nn(lhs, rhs):
    return lax.dot_general(lhs, rhs, (((1,), (0,)), ((), ())), preferred_element_type=jnp.float32)


def dot_nt(lhs, rhs):
    return lax.dot_general(lhs, rhs, (((1,), (1,)), ((), ())), preferred_element_type=jnp.float32)


def dot_tn(lhs, rhs):
    return lax.dot_general(lhs, rhs, (((0,), (0,)), ((), ())), preferred_element_type=jnp.float32)


def orders_low(plane_count):
    return np.arange(2 * plane_count * low_each).reshape(2, plane_count, low_each)


def orders_high(plane_count):
    first = 2 * plane_count * low_each
    return first + np.arange(high_each)[None, :] * plane_count + np.arange(plane_count)[:, None]


def fourier_tables(lon_count, plane_count):
    positions = np.arange(lon_count)

    def entries(orders):
        phase = (orders[..., None] * positions) % lon_count
        angles = phase.astype(np.float32) * np.float32(2.0 * math.pi / lon_count)
        factor = np.where(orders == 0, 1.0, 2.0).astype(np.float32)[..., None]
        plain = np.stack([np.cos(angles), -np.sin(angles)], axis=-2)
        return (plain * factor[..., None], plain)

    low = orders_low(plane_count)
    high = orders_high(plane_count)
    rows = plane_count * low_each * 2
    low_synth, low_plain = entries(low)
    high_synth, high_plain = entries(high)
    synth = np.concatenate(
        [low_synth.reshape(2, rows, lon_count), high_synth.reshape(1, rows, lon_count)]
    )
    analysis = np.concatenate(
        [low_plain.reshape(2, rows, lon_count), high_plain.reshape(1, rows, lon_count)]
    )
    analysis = analysis.transpose(0, 2, 1)
    return (
        jnp.asarray(synth.astype(ml_dtypes.bfloat16)),
        jnp.asarray(analysis.astype(ml_dtypes.bfloat16)),
    )


def latitude_tables(row_count, plane_count, total_lat):
    half = np.arange(2)[:, None, None, None]
    side = np.arange(2)[None, :, None, None]
    row = np.arange(row_count)[None, None, :, None]
    sender = np.arange(plane_count)[None, None, None, :]
    side_half = np.where(side == 0, half, 1 - half)
    lat_rows = ((side_half * plane_count + sender) * row_count + row).reshape(2, total_lat)
    angles = (lat_rows + 0.5) * (math.pi / total_lat)
    low = orders_low(plane_count)
    high = np.broadcast_to(orders_high(plane_count)[None], (2, plane_count, high_each))
    orders = np.concatenate([low, high], axis=2)
    factor_index = np.arange(1, total_lat + 1)
    ratios = np.log((2.0 * factor_index - 1.0) / (2.0 * factor_index))
    partial_log = np.concatenate([[0.0], np.cumsum(ratios)])[orders]
    start_log = (0.5 * np.log(orders + 0.5) + 0.5 * partial_log)[..., None] + orders[
        ..., None
    ] * np.log(np.sin(angles))[:, None, None, :]
    start_log = start_log.reshape(2 * plane_count, low_each + high_each, total_lat)
    cosine = np.broadcast_to(np.cos(angles)[:, None, :], (2, low_each + high_each, total_lat))
    quad = np.sin(angles) * (math.pi / total_lat)
    quad = np.broadcast_to(quad[:, :, None], (2, total_lat, 128))
    local = (np.arange(total_lat).reshape(2 * plane_count, row_count) + 0.5) * (math.pi / total_lat)
    area = np.zeros((2 * plane_count, 8, 128))
    area[:, :row_count, :] = np.sin(local)[:, :, None]
    return tuple(jnp.asarray(table.astype(np.float32)) for table in (start_log, cosine, quad, area))


def legendre_fill(block, start_ref, order_f, cosine_ref, rows_ref, table_ref, high_ref):
    degree_count = rows_ref.shape[0]
    cosine = cosine_ref[...]
    zeros = jnp.zeros(cosine.shape, jnp.float32)

    def advance_block(step, state):
        older, newer, log_scale = state
        half_scale = jnp.exp(0.5 * log_scale)
        for offset in range(block):
            degree = step * block + offset
            degree_f = degree.astype(jnp.float32)
            below = degree_f - 1.0
            alpha_rec = jnp.sqrt(
                jnp.maximum(4.0 * degree_f * degree_f - 1.0, 1.0)
                / jnp.maximum(degree_f * degree_f - order_f * order_f, 1.0)
            )
            beta_rec = jnp.sqrt(
                jnp.maximum(below * below - order_f * order_f, 0.0)
                / jnp.maximum(4.0 * below * below - 1.0, 1.0)
            )
            recurred = alpha_rec * (cosine * newer - beta_rec * older)
            fresh = jnp.where(
                degree_f < order_f, 0.0, jnp.where(degree_f == order_f, 1.0, recurred)
            )
            rows_ref[degree] = (fresh * half_scale) * half_scale
            older, newer = newer, fresh
        largest = jnp.maximum(jnp.abs(older), jnp.abs(newer))
        norm_value = jnp.where(largest > 0.0, largest, 1.0)
        return (older / norm_value, newer / norm_value, log_scale + jnp.log(norm_value))

    lax.fori_loop(0, degree_count // block, advance_block, (zeros, zeros, start_ref[...]))
    for slot in range(low_each):
        table_ref[slot] = rows_ref[:, slot, :].astype(jnp.bfloat16)
    for slot in range(high_each):
        kept = rows_ref[degree_count - high_ref.shape[1] :, low_each + slot, :]
        high_ref[slot] = kept[:, : high_ref.shape[2]].astype(jnp.bfloat16)


def fused_kernel(
    grid_all, saved_all, target_ref, land_ref, mix_ref, gain_ref, up_ref, down_ref,
    synth_all, analysis_all, start_all, cosine_all, quad_all, area_all,
    out_all,
    grid_ref, saved_ref, synth_ref, analysis_ref,
    own_target, start_ref, cosine_ref, quad_ref, area_ref, weight_rows, weight_ref, gain_low,
    gain_high,
    send_points, recv_points, send_cot, cot_ref, slopes_ref, mixed_ref,
    gather_own, gather_high, gather_other, gather_f32, gather_late,
    zsend, zrecv, psend, precv, wave_f32, rows_ref, table_ref, high_ref,
    wave_ref, coeff_ref, high_f32, high_send, high_recv, high_coeff, total_ref,
    rsend, rrecv, yown, yhigh, zsend_back, zrecv_back,
    local_sem, row_sem, point_ss, point_rs, cot_ss, cot_rs, z_ss, z_rs, p_ss, p_rs, r_ss, r_rs,
    zb_ss, zb_rs, h_ss, h_rs,
):
    row_count, lon_count, channels = saved_ref.shape
    member_count = recv_points.shape[0]
    part = lon_count // member_count
    plane_count = precv.shape[0]
    pair_count = precv.shape[1]
    piece = precv.shape[2]
    third = piece // 3
    keys = 2 * low_each
    own_lats = row_count * plane_count
    total_lat = 2 * own_lats
    region = (high_each + 1) * plane_count

    member = lax.axis_index("member")
    lat = lax.axis_index("lat")
    half = lat // plane_count
    spot = lat - half * plane_count
    partner = {"lat": lax.rem(lat + plane_count, 2 * plane_count)}

    def member_peer(step):
        return {"member": lax.rem(member + step, member_count)}

    cores = 2
    columns = min(4, plane_count // cores)
    lines = plane_count // (cores * columns)

    def plane_spot(step):
        shift = lax.rem(step * 19, plane_count)
        core = lax.rem(spot + shift, cores)
        column = lax.rem(spot // cores + shift // cores, columns)
        line = lax.rem(spot // (cores * columns) + shift // (cores * columns), lines)
        return (line * columns + column) * cores + core

    def plane_peer(step):
        return {"lat": half * plane_count + plane_spot(step)}

    barrier = pltpu.get_barrier_semaphore()
    for step in range(1, member_count):
        pl.semaphore_signal(barrier, inc=1, device_id=member_peer(step), device_id_type=MESH)
    pl.semaphore_signal(barrier, inc=1, device_id=partner, device_id_type=MESH)

    def greet(step, carry):
        pl.semaphore_signal(barrier, inc=1, device_id=plane_peer(step), device_id_type=MESH)
        return carry

    lax.fori_loop(1, plane_count, greet, 0)

    def row_copies(row):
        return [
            pltpu.make_async_copy(saved_all.at[row], saved_ref.at[row], row_sem.at[0, row]),
            pltpu.make_async_copy(grid_all.at[row], grid_ref.at[row], row_sem.at[1, row]),
        ]

    def out_copy(row):
        return pltpu.make_async_copy(saved_ref.at[row], out_all.at[row], row_sem.at[2, row])

    local_copies = [
        pltpu.make_async_copy(
            target_ref.at[:, pl.ds(member * part, part), :], own_target, local_sem.at[0]
        ),
        pltpu.make_async_copy(start_all.at[lat], start_ref, local_sem.at[1]),
        pltpu.make_async_copy(cosine_all.at[half], cosine_ref, local_sem.at[2]),
        pltpu.make_async_copy(quad_all.at[half], quad_ref, local_sem.at[3]),
        pltpu.make_async_copy(area_all.at[lat], area_ref, local_sem.at[4]),
        pltpu.make_async_copy(synth_all, synth_ref, local_sem.at[5]),
        pltpu.make_async_copy(analysis_all, analysis_ref, local_sem.at[6]),
    ]
    for copy in row_copies(0) + row_copies(1) + local_copies:
        copy.start()
    for row in range(2, row_count):
        for copy in row_copies(row):
            copy.start()

    def point_copy(row, step):
        return pltpu.make_async_remote_copy(
            src_ref=send_points.at[step - 1, row],
            dst_ref=recv_points.at[member_count - step, row],
            send_sem=point_ss.at[row, step - 1],
            recv_sem=point_rs.at[row, step - 1],
            device_id=member_peer(step),
            device_id_type=MESH,
        )

    def cot_copy(row, step):
        return pltpu.make_async_remote_copy(
            src_ref=send_cot.at[step - 1, row],
            dst_ref=cot_ref.at[row, pl.ds(member * part, part), :],
            send_sem=cot_ss.at[row, step - 1],
            recv_sem=cot_rs.at[row, step - 1],
            device_id=member_peer(step),
            device_id_type=MESH,
        )

    def z_copy(row):
        return pltpu.make_async_remote_copy(
            src_ref=zsend.at[row],
            dst_ref=zrecv.at[row],
            send_sem=z_ss.at[row],
            recv_sem=z_rs.at[row],
            device_id=partner,
            device_id_type=MESH,
        )

    def p_copy(pair, side, step):
        rows = pl.ds(0, 2 * third) if side == 0 else pl.ds(2 * third, third)
        return pltpu.make_async_remote_copy(
            src_ref=psend.at[pair, plane_spot(step), rows, :],
            dst_ref=precv.at[spot, pair, rows, :],
            send_sem=p_ss.at[pair, side, step],
            recv_sem=p_rs.at[pair, side, step],
            device_id=plane_peer(step),
            device_id_type=MESH,
        )

    def r_copy(index, step):
        if index < pair_count:
            slot, rows = 0, pl.ds(index * third, third)
        else:
            slot, rows = index - pair_count + 1, pl.ds(0, piece)
        return pltpu.make_async_remote_copy(
            src_ref=rsend.at[slot, plane_spot(step), rows, :],
            dst_ref=rrecv.at[slot, spot, rows, :],
            send_sem=r_ss.at[index, step],
            recv_sem=r_rs.at[index, step],
            device_id=plane_peer(step),
            device_id_type=MESH,
        )

    def zb_copy(pair):
        rows = pl.ds(pair * pair_rows, pair_rows)
        return pltpu.make_async_remote_copy(
            src_ref=zsend_back.at[rows],
            dst_ref=zrecv_back.at[rows],
            send_sem=zb_ss.at[pair],
            recv_sem=zb_rs.at[pair],
            device_id=partner,
            device_id_type=MESH,
        )

    def forward_part(row, step):
        begin = pl.multiple_of(lax.rem(member + step, member_count) * part, part)
        hidden_pre = dot_nn(saved_ref[row, pl.ds(begin, part), :], up_ref[...])
        values, slopes = gelu_parts(hidden_pre)
        slopes_ref[row, pl.ds(begin, part), :] = slopes.astype(jnp.bfloat16)
        branch = dot_nn(values.astype(jnp.bfloat16), down_ref[...])
        summed = grid_ref[row, pl.ds(begin, part), :].astype(jnp.float32) + branch
        return summed.astype(jnp.bfloat16)

    def forward_row(row):
        def one(step, carry):
            send_points[step - 1, row] = forward_part(row, step)
            point_copy(row, step).start()
            return carry

        for copy in row_copies(row):
            copy.wait()
        if row == 0:
            recv_points[0, row] = forward_part(row, 0)
            pl.semaphore_wait(barrier, member_count - 1 + 1 + plane_count - 1)
        lax.fori_loop(1, member_count, one, 0)
        if row > 0:
            recv_points[0, row] = forward_part(row, 0)

    def high_copy():
        theirs = pl.ds(pl.multiple_of((1 - half) * region, region), region)
        return pltpu.make_async_remote_copy(
            src_ref=high_send.at[theirs, :],
            dst_ref=high_recv,
            send_sem=h_ss.at[0],
            recv_sem=h_rs.at[0],
            device_id=partner,
            device_id_type=MESH,
        )

    def coeff_copy():
        mine = pl.ds(pl.multiple_of(half * region, region), region)
        return pltpu.make_async_remote_copy(
            src_ref=high_coeff.at[mine, :],
            dst_ref=high_coeff.at[mine, :],
            send_sem=h_ss.at[1],
            recv_sem=h_rs.at[1],
            device_id=partner,
            device_id_type=MESH,
        )

    strip = 16 if part % 16 == 0 else part

    def loss_row(row):
        for step in range(1, member_count):
            point_copy(row, step).wait_recv()
        own_begin = pl.multiple_of(member * part, part)

        def one(index, carry):
            begin = pl.multiple_of(index * strip, strip)
            here = pl.ds(begin, strip)
            values = [
                recv_points[slot, row, here, :].astype(jnp.float32) for slot in range(member_count)
            ]
            totals = [jnp.zeros(values[0].shape, jnp.float32) for slot in range(member_count)]
            for first in range(member_count):
                for second in range(first + 1, member_count):
                    slope = slope_abs(values[first] - values[second])
                    totals[first] = totals[first] + slope
                    totals[second] = totals[second] - slope
            wanted = own_target[row, here, :].astype(jnp.float32)
            spot_here = pl.ds(pl.multiple_of(own_begin + begin, strip), strip)
            weights = weight_ref[spot_here, row : row + 1]
            for slot in range(member_count):
                term = weights * (
                    slope_abs(values[slot] - wanted) / member_count
                    - totals[slot] / (member_count * member_count)
                )
                if slot == 0:
                    cot_ref[row, spot_here, :] = term.astype(jnp.bfloat16)
                else:
                    send_cot[slot - 1, row, here, :] = term.astype(jnp.bfloat16)
            return carry

        lax.fori_loop(0, part // strip, one, 0)
        for step in range(1, member_count):
            cot_copy(row, step).start()

    blocks, lane_width = gather_f32.shape[0], gather_f32.shape[2]

    def lanes_of(block):
        return slice(block * lane_width, (block + 1) * lane_width)

    def scatter_rows(target, first, count, stride, values):
        for block in range(blocks):
            target[block, pl.ds(first, count, stride=stride), :] = values[:, lanes_of(block)]

    def backward_row(row, own_slot):
        for step in range(1, member_count):
            cot_copy(row, step).wait_recv()

        def one(index, carry):
            here = pl.ds(pl.multiple_of(index * part, part), part)
            act_grad = dot_nt(cot_ref[row, here, :], down_ref[...])
            pre_grad = (act_grad * slopes_ref[row, here, :].astype(jnp.float32)).astype(jnp.bfloat16)
            mixed_ref[here, :] = dot_nt(pre_grad, up_ref[...]).astype(jnp.bfloat16)
            return carry

        lax.fori_loop(0, member_count, one, 0)
        other = dot_nn(synth_ref[1 - half], mixed_ref[...])
        zsend[row] = other.astype(jnp.bfloat16)
        z_copy(row).start()
        own = dot_nn(synth_ref[half], mixed_ref[...])
        scatter_rows(gather_own, own_slot, own.shape[0], pair_rows, own)
        high = dot_nn(synth_ref[2], mixed_ref[...])
        scatter_rows(gather_high, own_slot, high.shape[0], pair_rows, high)

    def pack(pair, first, source):
        for block in range(blocks):
            psend[pair, :, first : first + third, lanes_of(block)] = (
                source[block].reshape(plane_count, third, lane_width).astype(jnp.bfloat16)
            )

    def start_plane(pair, side):
        def one(step, carry):
            p_copy(pair, side, step).start()
            return carry

        lax.fori_loop(1, plane_count, one, 0)

    def own_pair(pair):
        pack(pair, 0, gather_high)
        pack(pair, third, gather_own)
        start_plane(pair, 0)
        precv[spot, pair, : 2 * third, :] = psend[pair, spot, : 2 * third, :]

    def other_pair(pair):
        for inner in range(pair_rows):
            row = pair * pair_rows + inner
            z_copy(row).wait_recv()
            scatter_rows(
                gather_other, inner, zrecv.shape[1], pair_rows, zrecv[row].astype(jnp.float32)
            )
        pack(pair, 2 * third, gather_other)
        start_plane(pair, 1)
        precv[spot, pair, 2 * third :, :] = psend[pair, spot, 2 * third :, :]

    group = pair_count * piece

    def await_pair(pair, side):
        def one(step, carry):
            p_copy(pair, side, step).wait_recv()
            return carry

        lax.fori_loop(1, plane_count, one, 0)
        begin, size = (0, 2 * third) if side == 0 else (2 * third, third)

        def widen(index, carry):
            here = pl.ds(pl.multiple_of(index * group + pair * piece + begin, third), size)
            for block in range(blocks):
                wave_f32[block, here, :] = precv[
                    index, pair, begin : begin + size, lanes_of(block)
                ].astype(jnp.float32)
            return carry

        lax.fori_loop(0, plane_count, widen, 0)

    def collect(first, begin, phase):
        for block in range(blocks):
            lane_begin = phase * channels + block * lane_width
            wave_ref[begin : begin + plane_count, lane_begin : lane_begin + lane_width] = wave_f32[
                block, pl.ds(first, plane_count, stride=group), :
            ].astype(jnp.bfloat16)

    def mix(gained):
        return jnp.concatenate(
            [
                dot_nt(gained[:, :channels], mix_ref[...]).astype(jnp.bfloat16),
                dot_nt(gained[:, channels:], mix_ref[...]).astype(jnp.bfloat16),
            ],
            axis=1,
        )

    def start_return(index):
        def one(step, carry):
            r_copy(index, step).start()
            return carry

        lax.fori_loop(1, plane_count, one, 0)

    def pack_return(slot, source):
        for block in range(blocks):
            rsend[slot, :, :, lanes_of(block)] = (
                source[block].reshape(plane_count, piece, lane_width).astype(jnp.bfloat16)
            )
        rrecv[slot, spot] = rsend[slot, spot]

    def await_return(index):
        def one(step, carry):
            r_copy(index, step).wait_recv()
            return carry

        lax.fori_loop(1, plane_count, one, 0)

    def low_analysis():
        def one_order(order, carry):
            for phase in range(2):
                key = order * 2 + phase
                for side in range(2):
                    for row in range(row_count):
                        first = (row // pair_rows) * piece + (1 + side) * third
                        first = first + key * pair_rows + row % pair_rows
                        collect(first, (side * row_count + row) * plane_count, phase)
            degree_grad = dot_nn(table_ref[order], wave_ref[...])
            coeff_ref[order] = mix((degree_grad * gain_low[:, 0:1]).astype(jnp.bfloat16))
            lat_grad = (
                dot_tn(table_ref[order, :, own_lats:], coeff_ref[order]) * quad_ref[own_lats:, 0:1]
            )
            for phase in range(2):
                for row in range(row_count):
                    first = (row // pair_rows) * third + (order * 2 + phase) * pair_rows
                    scatter_rows(
                        gather_f32,
                        first + row % pair_rows,
                        plane_count,
                        piece,
                        lat_grad[
                            row * plane_count : (row + 1) * plane_count,
                            phase * channels : (phase + 1) * channels,
                        ],
                    )
            return carry

        lax.fori_loop(0, low_each, one_order, 0)
        pack_return(0, gather_f32)
        for pair in range(pair_count):
            start_return(pair)

    def scatter_own(target, key, lat_grad):
        for phase in range(2):
            for row in range(row_count):
                scatter_rows(
                    target,
                    (key + phase) * row_count + row,
                    plane_count,
                    piece,
                    lat_grad[
                        row * plane_count : (row + 1) * plane_count,
                        phase * channels : (phase + 1) * channels,
                    ],
                )

    def low_own():
        def one_order(order, carry):
            lat_grad = (
                dot_tn(table_ref[order, :, :own_lats], coeff_ref[order]) * quad_ref[:own_lats, 0:1]
            )
            scatter_own(gather_late, order * 2, lat_grad)
            return carry

        lax.fori_loop(0, low_each, one_order, 0)
        pack_return(1, gather_late)
        start_return(pair_count)

    high_first = [0, 5 * plane_count, 8 * plane_count, 4 * plane_count]
    high_size = [(high_each - slot) * plane_count for slot in range(high_each)]

    def high_analysis():
        for slot in range(high_each):
            for phase in range(2):
                key = slot * 2 + phase
                for row in range(row_count):
                    first = (row // pair_rows) * piece + key * pair_rows + row % pair_rows
                    collect(first, row * plane_count, phase)
            here = slice(high_first[slot], high_first[slot] + high_size[slot])
            total = dot_nn(high_ref[slot, slot * plane_count :, :], wave_ref[:own_lats, :])
            high_f32[here, :] = total
            high_send[here, :] = total.astype(jnp.bfloat16)
        high_copy().start()

    def high_middle():
        high_copy().wait_recv()
        mine = pl.ds(pl.multiple_of(half * region, region), region)
        total = high_f32[mine, :] + high_recv[...].astype(jnp.float32)
        gained = (total * gain_high[mine, 0:1]).astype(jnp.bfloat16)
        high_coeff[mine, :] = mix(gained)
        coeff_copy().start()

    def high_synthesis():
        coeff_copy().wait_recv()
        for slot in range(high_each):
            here = slice(high_first[slot], high_first[slot] + high_size[slot])
            lat_grad = (
                dot_tn(high_ref[slot, slot * plane_count :, :], high_coeff[here, :])
                * quad_ref[:own_lats, 0:1]
            )
            scatter_own(gather_late, slot * 2, lat_grad)
        pack_return(2, gather_late)
        start_return(pair_count + 1)

    def return_pair(pair):
        await_return(pair)
        begin = pair * third
        for block in range(blocks):
            gather_other[block] = (
                rrecv[0, :, begin : begin + third, lanes_of(block)]
                .reshape(plane_count * third, lane_width)
                .astype(jnp.float32)
            )
        for inner in range(pair_rows):
            for block in range(blocks):
                zsend_back[pair * pair_rows + inner, :, lanes_of(block)] = gather_other[
                    block, pl.ds(inner, zsend_back.shape[1], stride=pair_rows), :
                ].astype(jnp.bfloat16)
        zb_copy(pair).start()

    def return_own(slot, target):
        await_return(pair_count + slot - 1)
        for block in range(blocks):
            gather_f32[block] = (
                rrecv[slot, :, :, lanes_of(block)]
                .reshape(plane_count * piece, lane_width)
                .astype(jnp.float32)
            )
        for row in range(row_count):
            for block in range(blocks):
                target[row, :, lanes_of(block)] = gather_f32[
                    block, pl.ds(row, target.shape[1], stride=row_count), :
                ].astype(jnp.bfloat16)

    forward_row(0)
    forward_row(1)
    forward_row(2)
    forward_row(3)
    for copy in local_copies:
        copy.wait()
    spread = lax.broadcasted_iota(jnp.int32, cosine_ref.shape, 0)
    low_order = half * (plane_count * low_each) + spot * low_each + spread
    high_order = 2 * plane_count * low_each + (spread - low_each) * plane_count + spot
    order_f = jnp.where(spread < low_each, low_order, high_order).astype(jnp.float32)
    weight_rows[...] = jnp.zeros(weight_rows.shape, jnp.float32)
    weight_rows[:row_count, :] = land_ref[...].astype(jnp.float32) * area_ref[:row_count, 0:1]
    weight_ref[...] = weight_rows[...].T
    gain_low[...] = jnp.broadcast_to(gain_ref[...], (8, total_lat)).T
    for slot in range(high_each):
        gain_high[high_first[slot] : high_first[slot] + high_size[slot], :] = gain_low[
            total_lat - high_size[slot] :, :
        ]
    legendre_fill(
        math.gcd(total_lat, 16), start_ref, order_f, cosine_ref, rows_ref, table_ref, high_ref
    )
    for row in range(row_count):
        loss_row(row)
        if row + 4 < row_count:
            forward_row(row + 4)
        if row >= 1:
            backward_row(row - 1, (row - 1) % pair_rows)
            if row % pair_rows == 0:
                own_pair(row // pair_rows - 1)
            elif row > pair_rows:
                other_pair(row // pair_rows - 1)
    backward_row(row_count - 1, (row_count - 1) % pair_rows)
    own_pair(pair_count - 1)
    for pair in range(pair_count - 1):
        await_pair(pair, 0)
        await_pair(pair, 1)
    other_pair(pair_count - 1)
    await_pair(pair_count - 1, 0)
    high_analysis()
    await_pair(pair_count - 1, 1)
    high_middle()
    low_analysis()
    high_synthesis()
    for pair in range(pair_count):
        return_pair(pair)
    low_own()
    return_own(2, yhigh)
    return_own(1, yown)

    def own_part(row, carry):
        total_ref[row] = dot_nn(analysis_ref[half], yown[row]) + dot_nn(analysis_ref[2], yhigh[row])
        return carry

    lax.fori_loop(0, row_count, own_part, 0)

    def finish(row, carry):
        spatial = total_ref[row] + dot_nn(analysis_ref[1 - half], zrecv_back[row])
        saved_ref[row] = (
            cot_ref[row].astype(jnp.float32) + spatial * (1.0 / lon_count)
        ).astype(jnp.bfloat16)
        out_copy(row).start()
        return carry

    for pair in range(pair_count):
        zb_copy(pair).wait_recv()
        lax.fori_loop(pair * pair_rows, (pair + 1) * pair_rows, finish, 0)

    def drain_rows(row, carry):
        for step in range(1, member_count):
            point_copy(row, step).wait_send()
            cot_copy(row, step).wait_send()
        z_copy(row).wait_send()
        return carry

    lax.fori_loop(0, row_count, drain_rows, 0)

    def drain_plane(step, carry):
        for pair in range(pair_count):
            p_copy(pair, 0, step).wait_send()
            p_copy(pair, 1, step).wait_send()
        for index in range(pair_count + 2):
            r_copy(index, step).wait_send()
        return carry

    lax.fori_loop(1, plane_count, drain_plane, 0)
    for pair in range(pair_count):
        zb_copy(pair).wait_send()
    high_copy().wait_send()
    coeff_copy().wait_send()
    for row in range(row_count):
        out_copy(row).wait()


def shards(
    grid_input, saved_mixed, target, land_weight, mix_weight, degree_gain, up_weight, down_weight
):
    row_count, lon_count, channels = grid_input.shape[1:]
    hidden = up_weight.shape[1]
    total_lat = degree_gain.shape[0]
    member_count = lax.axis_size("member")
    plane_count = lax.axis_size("lat") // 2
    part = lon_count // member_count
    pair_count = row_count // pair_rows
    keys = plane_count * 2 * low_each
    third = 2 * low_each * pair_rows
    piece = 3 * third
    order_slots = low_each + high_each
    region = (high_each + 1) * plane_count
    own_lats = row_count * plane_count
    synth, analysis = fourier_tables(lon_count, plane_count)
    start_log, cosine, quad, area = latitude_tables(row_count, plane_count, total_lat)

    blocks = max(channels // 128, 1)
    bf16 = jnp.bfloat16
    f32 = jnp.float32
    vmem = pl.BlockSpec(memory_space=pltpu.VMEM)
    anywhere = pl.BlockSpec(memory_space=pl.ANY)
    dma = pltpu.SemaphoreType.DMA
    result = pl.pallas_call(
        fused_kernel,
        out_shape=jax.ShapeDtypeStruct((row_count, lon_count, channels), bf16),
        in_specs=[anywhere] * 3 + [vmem] * 5 + [anywhere] * 6,
        out_specs=anywhere,
        scratch_shapes=[
            pltpu.VMEM((row_count, lon_count, channels), bf16),
            pltpu.VMEM((row_count, lon_count, channels), bf16),
            pltpu.VMEM(synth.shape, bf16),
            pltpu.VMEM(analysis.shape, bf16),
            pltpu.VMEM((row_count, part, channels), bf16),
            pltpu.VMEM((order_slots, total_lat), f32),
            pltpu.VMEM((order_slots, total_lat), f32),
            pltpu.VMEM((total_lat, 128), f32),
            pltpu.VMEM((8, 128), f32),
            pltpu.VMEM((8, lon_count), f32),
            pltpu.VMEM((lon_count, 8), f32),
            pltpu.VMEM((total_lat, 8), f32),
            pltpu.VMEM((2 * region, 8), f32),
            pltpu.VMEM((member_count - 1, row_count, part, channels), bf16),
            pltpu.VMEM((member_count, row_count, part, channels), bf16),
            pltpu.VMEM((member_count - 1, row_count, part, channels), bf16),
            pltpu.VMEM((row_count, lon_count, channels), bf16),
            pltpu.VMEM((row_count, lon_count, hidden), bf16),
            pltpu.VMEM((lon_count, channels), bf16),
            pltpu.VMEM((blocks, plane_count * third, channels // blocks), f32),
            pltpu.VMEM((blocks, plane_count * third, channels // blocks), f32),
            pltpu.VMEM((blocks, plane_count * third, channels // blocks), f32),
            pltpu.VMEM((blocks, plane_count * piece, channels // blocks), f32),
            pltpu.VMEM((blocks, plane_count * piece, channels // blocks), f32),
            pltpu.VMEM((row_count, keys, channels), bf16),
            pltpu.VMEM((row_count, keys, channels), bf16),
            pltpu.VMEM((pair_count, plane_count, piece, channels), bf16),
            pltpu.VMEM((plane_count, pair_count, piece, channels), bf16),
            pltpu.VMEM((blocks, plane_count * pair_count * piece, channels // blocks), f32),
            pltpu.VMEM((total_lat, order_slots, total_lat), f32),
            pltpu.VMEM((low_each, total_lat, total_lat), bf16),
            pltpu.VMEM((high_each, high_each * plane_count, own_lats), bf16),
            pltpu.VMEM((total_lat, 2 * channels), bf16),
            pltpu.VMEM((low_each, total_lat, 2 * channels), bf16),
            pltpu.VMEM((2 * region, 2 * channels), f32),
            pltpu.VMEM((2 * region, 2 * channels), bf16),
            pltpu.VMEM((region, 2 * channels), bf16),
            pltpu.VMEM((2 * region, 2 * channels), bf16),
            pltpu.VMEM((row_count, lon_count, channels), f32),
            pltpu.VMEM((3, plane_count, piece, channels), bf16),
            pltpu.VMEM((3, plane_count, piece, channels), bf16),
            pltpu.VMEM((row_count, keys, channels), bf16),
            pltpu.VMEM((row_count, keys, channels), bf16),
            pltpu.VMEM((row_count, keys, channels), bf16),
            pltpu.VMEM((row_count, keys, channels), bf16),
            dma((7,)),
            dma((3, row_count)),
            dma((row_count, member_count - 1)),
            dma((row_count, member_count - 1)),
            dma((row_count, member_count - 1)),
            dma((row_count, member_count - 1)),
            dma((row_count,)),
            dma((row_count,)),
            dma((pair_count, 2, plane_count)),
            dma((pair_count, 2, plane_count)),
            dma((pair_count + 2, plane_count)),
            dma((pair_count + 2, plane_count)),
            dma((pair_count,)),
            dma((pair_count,)),
            dma((2,)),
            dma((2,)),
        ],
        compiler_params=pltpu.CompilerParams(
            collective_id=0, has_side_effects=True, vmem_limit_bytes=63 * 2**20
        ),
    )(
        grid_input[0],
        saved_mixed[0],
        target,
        land_weight,
        mix_weight,
        degree_gain[None, :],
        up_weight,
        down_weight,
        synth,
        analysis,
        start_log,
        cosine,
        quad,
        area,
    )
    return result[None]


def solution(mesh):
    in_specs = (
        P("member", "lat", None, None),
        P("member", "lat", None, None),
        P("lat", None, None),
        P("lat", None),
        P(),
        P(),
        P(),
        P(),
    )
    out_specs = P("member", "lat", None, None)
    return jax.shard_map(shards, mesh=mesh, in_specs=in_specs, out_specs=out_specs, check_vma=False)
```

```python
import functools
import math

import jax
import jax.numpy as jnp
import ml_dtypes
import numpy as np
from jax import lax
from jax.experimental import pallas as pl
from jax.experimental.pallas import tpu as pltpu
from jax.sharding import PartitionSpec as P

kappa_gelu = 0.7978845608
cubic_gelu = 0.044715
smooth_square = 0.25
pair_rows = 2
low_each = 4
high_each = 4
MESH = pl.DeviceIdType.MESH


def gelu_parts(inputs):
    squared = inputs * inputs
    tanh_part = jnp.tanh(kappa_gelu * inputs * (1.0 + cubic_gelu * squared))
    half_sum = 0.5 * (1.0 + tanh_part)
    values = inputs * half_sum
    slopes = half_sum + 0.5 * inputs * (1.0 - tanh_part * tanh_part) * (
        kappa_gelu + (3.0 * cubic_gelu * kappa_gelu) * squared
    )
    return (values, slopes)


def slope_abs(difference):
    return difference * lax.rsqrt(difference * difference + smooth_square)


def dot_nn(lhs, rhs):
    return lax.dot_general(lhs, rhs, (((1,), (0,)), ((), ())), preferred_element_type=jnp.float32)


def dot_nt(lhs, rhs):
    return lax.dot_general(lhs, rhs, (((1,), (1,)), ((), ())), preferred_element_type=jnp.float32)


def dot_tn(lhs, rhs):
    return lax.dot_general(lhs, rhs, (((0,), (0,)), ((), ())), preferred_element_type=jnp.float32)


def orders_low(plane_count):
    return np.arange(2 * plane_count * low_each).reshape(2, plane_count, low_each)


def orders_high(plane_count):
    first = 2 * plane_count * low_each
    return first + np.arange(high_each)[None, :] * plane_count + np.arange(plane_count)[:, None]


def fourier_tables(lon_count, plane_count):
    positions = np.arange(lon_count)

    def entries(orders):
        phase = (orders[..., None] * positions) % lon_count
        angles = phase.astype(np.float32) * np.float32(2.0 * math.pi / lon_count)
        factor = np.where(orders == 0, 1.0, 2.0).astype(np.float32)[..., None]
        plain = np.stack([np.cos(angles), -np.sin(angles)], axis=-2)
        return (plain * factor[..., None], plain)

    low = orders_low(plane_count)
    high = orders_high(plane_count)
    rows = plane_count * low_each * 2
    low_synth, low_plain = entries(low)
    high_synth, high_plain = entries(high)
    synth = np.concatenate(
        [low_synth.reshape(2, rows, lon_count), high_synth.reshape(1, rows, lon_count)]
    )
    analysis = np.concatenate(
        [low_plain.reshape(2, rows, lon_count), high_plain.reshape(1, rows, lon_count)]
    )
    analysis = analysis.transpose(0, 2, 1)
    return (
        jnp.asarray(synth.astype(ml_dtypes.bfloat16)),
        jnp.asarray(analysis.astype(ml_dtypes.bfloat16)),
    )


def latitude_tables(row_count, plane_count, total_lat):
    half = np.arange(2)[:, None, None, None]
    side = np.arange(2)[None, :, None, None]
    row = np.arange(row_count)[None, None, :, None]
    sender = np.arange(plane_count)[None, None, None, :]
    side_half = np.where(side == 0, half, 1 - half)
    lat_rows = ((side_half * plane_count + sender) * row_count + row).reshape(2, total_lat)
    angles = (lat_rows + 0.5) * (math.pi / total_lat)
    low = orders_low(plane_count)
    high = np.broadcast_to(orders_high(plane_count)[None], (2, plane_count, high_each))
    orders = np.concatenate([low, high], axis=2)
    factor_index = np.arange(1, total_lat + 1)
    ratios = np.log((2.0 * factor_index - 1.0) / (2.0 * factor_index))
    partial_log = np.concatenate([[0.0], np.cumsum(ratios)])[orders]
    start_log = (0.5 * np.log(orders + 0.5) + 0.5 * partial_log)[..., None] + orders[
        ..., None
    ] * np.log(np.sin(angles))[:, None, None, :]
    start_log = start_log.reshape(2 * plane_count, low_each + high_each, total_lat)
    cosine = np.broadcast_to(np.cos(angles)[:, None, :], (2, low_each + high_each, total_lat))
    quad = np.sin(angles) * (math.pi / total_lat)
    quad = np.broadcast_to(quad[:, :, None], (2, total_lat, 128))
    local = (np.arange(total_lat).reshape(2 * plane_count, row_count) + 0.5) * (math.pi / total_lat)
    area = np.zeros((2 * plane_count, 8, 128))
    area[:, :row_count, :] = np.sin(local)[:, :, None]
    return tuple(jnp.asarray(table.astype(np.float32)) for table in (start_log, cosine, quad, area))


def legendre_fill(block, start_ref, order_f, cosine_ref, rows_ref, table_ref, high_ref):
    degree_count = rows_ref.shape[0]
    cosine = cosine_ref[...]
    zeros = jnp.zeros(cosine.shape, jnp.float32)

    def advance_block(step, state):
        older, newer, log_scale = state
        half_scale = jnp.exp(0.5 * log_scale)
        for offset in range(block):
            degree = step * block + offset
            degree_f = degree.astype(jnp.float32)
            below = degree_f - 1.0
            alpha_rec = jnp.sqrt(
                jnp.maximum(4.0 * degree_f * degree_f - 1.0, 1.0)
                / jnp.maximum(degree_f * degree_f - order_f * order_f, 1.0)
            )
            beta_rec = jnp.sqrt(
                jnp.maximum(below * below - order_f * order_f, 0.0)
                / jnp.maximum(4.0 * below * below - 1.0, 1.0)
            )
            recurred = alpha_rec * (cosine * newer - beta_rec * older)
            fresh = jnp.where(
                degree_f < order_f, 0.0, jnp.where(degree_f == order_f, 1.0, recurred)
            )
            rows_ref[degree] = (fresh * half_scale) * half_scale
            older, newer = newer, fresh
        largest = jnp.maximum(jnp.abs(older), jnp.abs(newer))
        norm_value = jnp.where(largest > 0.0, largest, 1.0)
        return (older / norm_value, newer / norm_value, log_scale + jnp.log(norm_value))

    lax.fori_loop(0, degree_count // block, advance_block, (zeros, zeros, start_ref[...]))
    for slot in range(low_each):
        table_ref[slot] = rows_ref[:, slot, :].astype(jnp.bfloat16)
    for slot in range(high_each):
        kept = rows_ref[degree_count - high_ref.shape[1] :, low_each + slot, :]
        high_ref[slot] = kept[:, : high_ref.shape[2]].astype(jnp.bfloat16)


def fused_kernel(
    grid_all, saved_all, target_ref, land_ref, mix_ref, gain_ref, up_ref, down_ref,
    synth_all, analysis_all, start_all, cosine_all, quad_all, area_all,
    out_all,
    grid_ref, saved_ref, synth_ref, analysis_ref,
    own_target, start_ref, cosine_ref, quad_ref, area_ref, weight_rows, weight_ref, gain_low,
    gain_high,
    send_points, recv_points, send_cot, cot_ref, slopes_ref, mixed_ref,
    gather_own, gather_high, gather_other, gather_f32, gather_late,
    zsend, zrecv, psend, precv, wave_f32, rows_ref, table_ref, high_ref,
    wave_ref, coeff_ref, high_f32, high_send, high_recv, high_coeff, total_ref,
    rsend, rrecv, yown, yhigh, zsend_back, zrecv_back,
    local_sem, row_sem, point_ss, point_rs, cot_ss, cot_rs, z_ss, z_rs, p_ss, p_rs, r_ss, r_rs,
    zb_ss, zb_rs, h_ss, h_rs,
):
    row_count, lon_count, channels = saved_ref.shape
    member_count = recv_points.shape[0]
    part = lon_count // member_count
    plane_count = precv.shape[0]
    pair_count = precv.shape[1]
    piece = precv.shape[2]
    third = piece // 3
    keys = 2 * low_each
    own_lats = row_count * plane_count
    total_lat = 2 * own_lats
    region = (high_each + 1) * plane_count

    member = lax.axis_index("member")
    lat = lax.axis_index("lat")
    half = lat // plane_count
    spot = lat - half * plane_count
    partner = {"lat": lax.rem(lat + plane_count, 2 * plane_count)}

    def member_peer(step):
        return {"member": lax.rem(member + step, member_count)}

    cores = 2
    columns = min(4, plane_count // cores)
    lines = plane_count // (cores * columns)

    def plane_spot(step):
        shift = lax.rem(step * 19, plane_count)
        core = lax.rem(spot + shift, cores)
        column = lax.rem(spot // cores + shift // cores, columns)
        line = lax.rem(spot // (cores * columns) + shift // (cores * columns), lines)
        return (line * columns + column) * cores + core

    def plane_peer(step):
        return {"lat": half * plane_count + plane_spot(step)}

    barrier = pltpu.get_barrier_semaphore()
    for step in range(1, member_count):
        pl.semaphore_signal(barrier, inc=1, device_id=member_peer(step), device_id_type=MESH)
    pl.semaphore_signal(barrier, inc=1, device_id=partner, device_id_type=MESH)

    def greet(step, carry):
        pl.semaphore_signal(barrier, inc=1, device_id=plane_peer(step), device_id_type=MESH)
        return carry

    lax.fori_loop(1, plane_count, greet, 0)

    def row_copies(row):
        return [
            pltpu.make_async_copy(saved_all.at[row], saved_ref.at[row], row_sem.at[0, row]),
            pltpu.make_async_copy(grid_all.at[row], grid_ref.at[row], row_sem.at[1, row]),
        ]

    def out_copy(row):
        return pltpu.make_async_copy(saved_ref.at[row], out_all.at[row], row_sem.at[2, row])

    local_copies = [
        pltpu.make_async_copy(
            target_ref.at[:, pl.ds(member * part, part), :], own_target, local_sem.at[0]
        ),
        pltpu.make_async_copy(start_all.at[lat], start_ref, local_sem.at[1]),
        pltpu.make_async_copy(cosine_all.at[half], cosine_ref, local_sem.at[2]),
        pltpu.make_async_copy(quad_all.at[half], quad_ref, local_sem.at[3]),
        pltpu.make_async_copy(area_all.at[lat], area_ref, local_sem.at[4]),
        pltpu.make_async_copy(synth_all, synth_ref, local_sem.at[5]),
        pltpu.make_async_copy(analysis_all, analysis_ref, local_sem.at[6]),
    ]
    for copy in row_copies(0) + row_copies(1) + local_copies:
        copy.start()
    for row in range(2, row_count):
        for copy in row_copies(row):
            copy.start()

    def point_copy(row, step):
        return pltpu.make_async_remote_copy(
            src_ref=send_points.at[step - 1, row],
            dst_ref=recv_points.at[member_count - step, row],
            send_sem=point_ss.at[row, step - 1],
            recv_sem=point_rs.at[row, step - 1],
            device_id=member_peer(step),
            device_id_type=MESH,
        )

    def cot_copy(row, step):
        return pltpu.make_async_remote_copy(
            src_ref=send_cot.at[step - 1, row],
            dst_ref=cot_ref.at[row, pl.ds(member * part, part), :],
            send_sem=cot_ss.at[row, step - 1],
            recv_sem=cot_rs.at[row, step - 1],
            device_id=member_peer(step),
            device_id_type=MESH,
        )

    def z_copy(row):
        return pltpu.make_async_remote_copy(
            src_ref=zsend.at[row],
            dst_ref=zrecv.at[row],
            send_sem=z_ss.at[row],
            recv_sem=z_rs.at[row],
            device_id=partner,
            device_id_type=MESH,
        )

    def p_copy(pair, side, step):
        rows = pl.ds(0, 2 * third) if side == 0 else pl.ds(2 * third, third)
        return pltpu.make_async_remote_copy(
            src_ref=psend.at[pair, plane_spot(step), rows, :],
            dst_ref=precv.at[spot, pair, rows, :],
            send_sem=p_ss.at[pair, side, step],
            recv_sem=p_rs.at[pair, side, step],
            device_id=plane_peer(step),
            device_id_type=MESH,
        )

    def r_copy(index, step):
        if index < pair_count:
            slot, rows = 0, pl.ds(index * third, third)
        else:
            slot, rows = index - pair_count + 1, pl.ds(0, piece)
        return pltpu.make_async_remote_copy(
            src_ref=rsend.at[slot, plane_spot(step), rows, :],
            dst_ref=rrecv.at[slot, spot, rows, :],
            send_sem=r_ss.at[index, step],
            recv_sem=r_rs.at[index, step],
            device_id=plane_peer(step),
            device_id_type=MESH,
        )

    def zb_copy(pair):
        rows = pl.ds(pair * pair_rows, pair_rows)
        return pltpu.make_async_remote_copy(
            src_ref=zsend_back.at[rows],
            dst_ref=zrecv_back.at[rows],
            send_sem=zb_ss.at[pair],
            recv_sem=zb_rs.at[pair],
            device_id=partner,
            device_id_type=MESH,
        )

    def forward_part(row, step):
        begin = pl.multiple_of(lax.rem(member + step, member_count) * part, part)
        hidden_pre = dot_nn(saved_ref[row, pl.ds(begin, part), :], up_ref[...])
        values, slopes = gelu_parts(hidden_pre)
        slopes_ref[row, pl.ds(begin, part), :] = slopes.astype(jnp.bfloat16)
        branch = dot_nn(values.astype(jnp.bfloat16), down_ref[...])
        summed = grid_ref[row, pl.ds(begin, part), :].astype(jnp.float32) + branch
        return summed.astype(jnp.bfloat16)

    def forward_row(row):
        def one(step, carry):
            send_points[step - 1, row] = forward_part(row, step)
            point_copy(row, step).start()
            return carry

        for copy in row_copies(row):
            copy.wait()
        if row == 0:
            recv_points[0, row] = forward_part(row, 0)
            pl.semaphore_wait(barrier, member_count - 1 + 1 + plane_count - 1)
        lax.fori_loop(1, member_count, one, 0)
        if row > 0:
            recv_points[0, row] = forward_part(row, 0)

    def high_copy():
        theirs = pl.ds(pl.multiple_of((1 - half) * region, region), region)
        return pltpu.make_async_remote_copy(
            src_ref=high_send.at[theirs, :],
            dst_ref=high_recv,
            send_sem=h_ss.at[0],
            recv_sem=h_rs.at[0],
            device_id=partner,
            device_id_type=MESH,
        )

    def coeff_copy():
        mine = pl.ds(pl.multiple_of(half * region, region), region)
        return pltpu.make_async_remote_copy(
            src_ref=high_coeff.at[mine, :],
            dst_ref=high_coeff.at[mine, :],
            send_sem=h_ss.at[1],
            recv_sem=h_rs.at[1],
            device_id=partner,
            device_id_type=MESH,
        )

    strip = 16 if part % 16 == 0 else part

    def loss_row(row):
        for step in range(1, member_count):
            point_copy(row, step).wait_recv()
        own_begin = pl.multiple_of(member * part, part)

        def one(index, carry):
            begin = pl.multiple_of(index * strip, strip)
            here = pl.ds(begin, strip)
            values = [
                recv_points[slot, row, here, :].astype(jnp.float32) for slot in range(member_count)
            ]
            totals = [jnp.zeros(values[0].shape, jnp.float32) for slot in range(member_count)]
            for first in range(member_count):
                for second in range(first + 1, member_count):
                    slope = slope_abs(values[first] - values[second])
                    totals[first] = totals[first] + slope
                    totals[second] = totals[second] - slope
            wanted = own_target[row, here, :].astype(jnp.float32)
            spot_here = pl.ds(pl.multiple_of(own_begin + begin, strip), strip)
            weights = weight_ref[spot_here, row : row + 1]
            for slot in range(member_count):
                term = weights * (
                    slope_abs(values[slot] - wanted) / member_count
                    - totals[slot] / (member_count * member_count)
                )
                if slot == 0:
                    cot_ref[row, spot_here, :] = term.astype(jnp.bfloat16)
                else:
                    send_cot[slot - 1, row, here, :] = term.astype(jnp.bfloat16)
            return carry

        lax.fori_loop(0, part // strip, one, 0)
        for step in range(1, member_count):
            cot_copy(row, step).start()

    blocks, lane_width = gather_f32.shape[0], gather_f32.shape[2]

    def lanes_of(block):
        return slice(block * lane_width, (block + 1) * lane_width)

    def scatter_rows(target, first, count, stride, values):
        for block in range(blocks):
            target[block, pl.ds(first, count, stride=stride), :] = values[:, lanes_of(block)]

    def backward_row(row, own_slot):
        for step in range(1, member_count):
            cot_copy(row, step).wait_recv()

        def one(index, carry):
            here = pl.ds(pl.multiple_of(index * part, part), part)
            act_grad = dot_nt(cot_ref[row, here, :], down_ref[...])
            pre_grad = (act_grad * slopes_ref[row, here, :].astype(jnp.float32)).astype(jnp.bfloat16)
            mixed_ref[here, :] = dot_nt(pre_grad, up_ref[...]).astype(jnp.bfloat16)
            return carry

        lax.fori_loop(0, member_count, one, 0)
        other = dot_nn(synth_ref[1 - half], mixed_ref[...])
        zsend[row] = other.astype(jnp.bfloat16)
        z_copy(row).start()
        own = dot_nn(synth_ref[half], mixed_ref[...])
        scatter_rows(gather_own, own_slot, own.shape[0], pair_rows, own)
        high = dot_nn(synth_ref[2], mixed_ref[...])
        scatter_rows(gather_high, own_slot, high.shape[0], pair_rows, high)

    def pack(pair, first, source):
        for block in range(blocks):
            psend[pair, :, first : first + third, lanes_of(block)] = (
                source[block].reshape(plane_count, third, lane_width).astype(jnp.bfloat16)
            )

    def start_plane(pair, side):
        def one(step, carry):
            p_copy(pair, side, step).start()
            return carry

        lax.fori_loop(1, plane_count, one, 0)

    def own_pair(pair):
        pack(pair, 0, gather_high)
        pack(pair, third, gather_own)
        start_plane(pair, 0)
        precv[spot, pair, : 2 * third, :] = psend[pair, spot, : 2 * third, :]

    def other_pair(pair):
        for inner in range(pair_rows):
            row = pair * pair_rows + inner
            z_copy(row).wait_recv()
            scatter_rows(
                gather_other, inner, zrecv.shape[1], pair_rows, zrecv[row].astype(jnp.float32)
            )
        pack(pair, 2 * third, gather_other)
        start_plane(pair, 1)
        precv[spot, pair, 2 * third :, :] = psend[pair, spot, 2 * third :, :]

    group = pair_count * piece

    def await_pair(pair, side):
        def one(step, carry):
            p_copy(pair, side, step).wait_recv()
            return carry

        lax.fori_loop(1, plane_count, one, 0)
        begin, size = (0, 2 * third) if side == 0 else (2 * third, third)

        def widen(index, carry):
            here = pl.ds(pl.multiple_of(index * group + pair * piece + begin, third), size)
            for block in range(blocks):
                wave_f32[block, here, :] = precv[
                    index, pair, begin : begin + size, lanes_of(block)
                ].astype(jnp.float32)
            return carry

        lax.fori_loop(0, plane_count, widen, 0)

    def collect(first, begin, phase):
        for block in range(blocks):
            lane_begin = phase * channels + block * lane_width
            wave_ref[begin : begin + plane_count, lane_begin : lane_begin + lane_width] = wave_f32[
                block, pl.ds(first, plane_count, stride=group), :
            ].astype(jnp.bfloat16)

    def mix(gained):
        return jnp.concatenate(
            [
                dot_nt(gained[:, :channels], mix_ref[...]).astype(jnp.bfloat16),
                dot_nt(gained[:, channels:], mix_ref[...]).astype(jnp.bfloat16),
            ],
            axis=1,
        )

    def start_return(index):
        def one(step, carry):
            r_copy(index, step).start()
            return carry

        lax.fori_loop(1, plane_count, one, 0)

    def pack_return(slot, source):
        for block in range(blocks):
            rsend[slot, :, :, lanes_of(block)] = (
                source[block].reshape(plane_count, piece, lane_width).astype(jnp.bfloat16)
            )
        rrecv[slot, spot] = rsend[slot, spot]

    def await_return(index):
        def one(step, carry):
            r_copy(index, step).wait_recv()
            return carry

        lax.fori_loop(1, plane_count, one, 0)

    def low_analysis():
        def one_order(order, carry):
            for phase in range(2):
                key = order * 2 + phase
                for side in range(2):
                    for row in range(row_count):
                        first = (row // pair_rows) * piece + (1 + side) * third
                        first = first + key * pair_rows + row % pair_rows
                        collect(first, (side * row_count + row) * plane_count, phase)
            degree_grad = dot_nn(table_ref[order], wave_ref[...])
            coeff_ref[order] = mix((degree_grad * gain_low[:, 0:1]).astype(jnp.bfloat16))
            lat_grad = (
                dot_tn(table_ref[order, :, own_lats:], coeff_ref[order]) * quad_ref[own_lats:, 0:1]
            )
            for phase in range(2):
                for row in range(row_count):
                    first = (row // pair_rows) * third + (order * 2 + phase) * pair_rows
                    scatter_rows(
                        gather_f32,
                        first + row % pair_rows,
                        plane_count,
                        piece,
                        lat_grad[
                            row * plane_count : (row + 1) * plane_count,
                            phase * channels : (phase + 1) * channels,
                        ],
                    )
            return carry

        lax.fori_loop(0, low_each, one_order, 0)
        pack_return(0, gather_f32)
        for pair in range(pair_count):
            start_return(pair)

    def scatter_own(target, key, lat_grad):
        for phase in range(2):
            for row in range(row_count):
                scatter_rows(
                    target,
                    (key + phase) * row_count + row,
                    plane_count,
                    piece,
                    lat_grad[
                        row * plane_count : (row + 1) * plane_count,
                        phase * channels : (phase + 1) * channels,
                    ],
                )

    def low_own():
        def one_order(order, carry):
            lat_grad = (
                dot_tn(table_ref[order, :, :own_lats], coeff_ref[order]) * quad_ref[:own_lats, 0:1]
            )
            scatter_own(gather_late, order * 2, lat_grad)
            return carry

        lax.fori_loop(0, low_each, one_order, 0)
        pack_return(1, gather_late)
        start_return(pair_count)

    high_first = [0, 5 * plane_count, 8 * plane_count, 4 * plane_count]
    high_size = [(high_each - slot) * plane_count for slot in range(high_each)]

    def high_analysis():
        for slot in range(high_each):
            for phase in range(2):
                key = slot * 2 + phase
                for row in range(row_count):
                    first = (row // pair_rows) * piece + key * pair_rows + row % pair_rows
                    collect(first, row * plane_count, phase)
            here = slice(high_first[slot], high_first[slot] + high_size[slot])
            total = dot_nn(high_ref[slot, slot * plane_count :, :], wave_ref[:own_lats, :])
            high_f32[here, :] = total
            high_send[here, :] = total.astype(jnp.bfloat16)
        high_copy().start()

    def high_middle():
        high_copy().wait_recv()
        mine = pl.ds(pl.multiple_of(half * region, region), region)
        total = high_f32[mine, :] + high_recv[...].astype(jnp.float32)
        gained = (total * gain_high[mine, 0:1]).astype(jnp.bfloat16)
        high_coeff[mine, :] = mix(gained)
        coeff_copy().start()

    def high_synthesis():
        coeff_copy().wait_recv()
        for slot in range(high_each):
            here = slice(high_first[slot], high_first[slot] + high_size[slot])
            lat_grad = (
                dot_tn(high_ref[slot, slot * plane_count :, :], high_coeff[here, :])
                * quad_ref[:own_lats, 0:1]
            )
            scatter_own(gather_late, slot * 2, lat_grad)
        pack_return(2, gather_late)
        start_return(pair_count + 1)

    def return_pair(pair):
        await_return(pair)
        begin = pair * third
        for block in range(blocks):
            gather_other[block] = (
                rrecv[0, :, begin : begin + third, lanes_of(block)]
                .reshape(plane_count * third, lane_width)
                .astype(jnp.float32)
            )
        for inner in range(pair_rows):
            for block in range(blocks):
                zsend_back[pair * pair_rows + inner, :, lanes_of(block)] = gather_other[
                    block, pl.ds(inner, zsend_back.shape[1], stride=pair_rows), :
                ].astype(jnp.bfloat16)
        zb_copy(pair).start()

    def return_own(slot, target):
        await_return(pair_count + slot - 1)
        for block in range(blocks):
            gather_f32[block] = (
                rrecv[slot, :, :, lanes_of(block)]
                .reshape(plane_count * piece, lane_width)
                .astype(jnp.float32)
            )
        for row in range(row_count):
            for block in range(blocks):
                target[row, :, lanes_of(block)] = gather_f32[
                    block, pl.ds(row, target.shape[1], stride=row_count), :
                ].astype(jnp.bfloat16)

    forward_row(0)
    forward_row(1)
    forward_row(2)
    forward_row(3)
    for copy in local_copies:
        copy.wait()
    spread = lax.broadcasted_iota(jnp.int32, cosine_ref.shape, 0)
    low_order = half * (plane_count * low_each) + spot * low_each + spread
    high_order = 2 * plane_count * low_each + (spread - low_each) * plane_count + spot
    order_f = jnp.where(spread < low_each, low_order, high_order).astype(jnp.float32)
    weight_rows[...] = jnp.zeros(weight_rows.shape, jnp.float32)
    weight_rows[:row_count, :] = land_ref[...].astype(jnp.float32) * area_ref[:row_count, 0:1]
    weight_ref[...] = weight_rows[...].T
    gain_low[...] = jnp.broadcast_to(gain_ref[...][None, :], (8, total_lat)).T
    for slot in range(high_each):
        gain_high[high_first[slot] : high_first[slot] + high_size[slot], :] = gain_low[
            total_lat - high_size[slot] :, :
        ]
    legendre_fill(
        math.gcd(total_lat, 16), start_ref, order_f, cosine_ref, rows_ref, table_ref, high_ref
    )
    for row in range(row_count):
        loss_row(row)
        if row + 4 < row_count:
            forward_row(row + 4)
        if row >= 1:
            backward_row(row - 1, (row - 1) % pair_rows)
            if row % pair_rows == 0:
                own_pair(row // pair_rows - 1)
            elif row > pair_rows:
                other_pair(row // pair_rows - 1)
    backward_row(row_count - 1, (row_count - 1) % pair_rows)
    own_pair(pair_count - 1)
    for pair in range(pair_count - 1):
        await_pair(pair, 0)
        await_pair(pair, 1)
    other_pair(pair_count - 1)
    await_pair(pair_count - 1, 0)
    high_analysis()
    await_pair(pair_count - 1, 1)
    high_middle()
    low_analysis()
    high_synthesis()
    for pair in range(pair_count):
        return_pair(pair)
    low_own()
    return_own(2, yhigh)
    return_own(1, yown)

    def own_part(row, carry):
        total_ref[row] = dot_nn(analysis_ref[half], yown[row]) + dot_nn(analysis_ref[2], yhigh[row])
        return carry

    lax.fori_loop(0, row_count, own_part, 0)

    def finish(row, carry):
        spatial = total_ref[row] + dot_nn(analysis_ref[1 - half], zrecv_back[row])
        saved_ref[row] = (
            cot_ref[row].astype(jnp.float32) + spatial * (1.0 / lon_count)
        ).astype(jnp.bfloat16)
        out_copy(row).start()
        return carry

    for pair in range(pair_count):
        zb_copy(pair).wait_recv()
        lax.fori_loop(pair * pair_rows, (pair + 1) * pair_rows, finish, 0)

    def drain_rows(row, carry):
        for step in range(1, member_count):
            point_copy(row, step).wait_send()
            cot_copy(row, step).wait_send()
        z_copy(row).wait_send()
        return carry

    lax.fori_loop(0, row_count, drain_rows, 0)

    def drain_plane(step, carry):
        for pair in range(pair_count):
            p_copy(pair, 0, step).wait_send()
            p_copy(pair, 1, step).wait_send()
        for index in range(pair_count + 2):
            r_copy(index, step).wait_send()
        return carry

    lax.fori_loop(1, plane_count, drain_plane, 0)
    for pair in range(pair_count):
        zb_copy(pair).wait_send()
    high_copy().wait_send()
    coeff_copy().wait_send()
    for row in range(row_count):
        out_copy(row).wait()


def shards(
    grid_input, saved_mixed, target, land_weight, mix_weight, degree_gain, up_weight, down_weight
):
    row_count, lon_count, channels = grid_input.shape[1:]
    hidden = up_weight.shape[1]
    total_lat = degree_gain.shape[0]
    member_count = lax.axis_size("member")
    plane_count = lax.axis_size("lat") // 2
    part = lon_count // member_count
    pair_count = row_count // pair_rows
    keys = plane_count * 2 * low_each
    third = 2 * low_each * pair_rows
    piece = 3 * third
    order_slots = low_each + high_each
    region = (high_each + 1) * plane_count
    own_lats = row_count * plane_count
    synth, analysis = fourier_tables(lon_count, plane_count)
    start_log, cosine, quad, area = latitude_tables(row_count, plane_count, total_lat)

    blocks = max(channels // 128, 1)
    bf16 = jnp.bfloat16
    f32 = jnp.float32
    vmem = pl.BlockSpec(memory_space=pltpu.VMEM)
    anywhere = pl.BlockSpec(memory_space=pl.ANY)
    dma = pltpu.SemaphoreType.DMA
    result = pl.pallas_call(
        fused_kernel,
        out_shape=jax.ShapeDtypeStruct((row_count, lon_count, channels), bf16),
        in_specs=[anywhere] * 3 + [vmem] * 5 + [anywhere] * 6,
        out_specs=anywhere,
        scratch_shapes=[
            pltpu.VMEM((row_count, lon_count, channels), bf16),
            pltpu.VMEM((row_count, lon_count, channels), bf16),
            pltpu.VMEM(synth.shape, bf16),
            pltpu.VMEM(analysis.shape, bf16),
            pltpu.VMEM((row_count, part, channels), bf16),
            pltpu.VMEM((order_slots, total_lat), f32),
            pltpu.VMEM((order_slots, total_lat), f32),
            pltpu.VMEM((total_lat, 128), f32),
            pltpu.VMEM((8, 128), f32),
            pltpu.VMEM((8, lon_count), f32),
            pltpu.VMEM((lon_count, 8), f32),
            pltpu.VMEM((total_lat, 8), f32),
            pltpu.VMEM((2 * region, 8), f32),
            pltpu.VMEM((member_count - 1, row_count, part, channels), bf16),
            pltpu.VMEM((member_count, row_count, part, channels), bf16),
            pltpu.VMEM((member_count - 1, row_count, part, channels), bf16),
            pltpu.VMEM((row_count, lon_count, channels), bf16),
            pltpu.VMEM((row_count, lon_count, hidden), bf16),
            pltpu.VMEM((lon_count, channels), bf16),
            pltpu.VMEM((blocks, plane_count * third, channels // blocks), f32),
            pltpu.VMEM((blocks, plane_count * third, channels // blocks), f32),
            pltpu.VMEM((blocks, plane_count * third, channels // blocks), f32),
            pltpu.VMEM((blocks, plane_count * piece, channels // blocks), f32),
            pltpu.VMEM((blocks, plane_count * piece, channels // blocks), f32),
            pltpu.VMEM((row_count, keys, channels), bf16),
            pltpu.VMEM((row_count, keys, channels), bf16),
            pltpu.VMEM((pair_count, plane_count, piece, channels), bf16),
            pltpu.VMEM((plane_count, pair_count, piece, channels), bf16),
            pltpu.VMEM((blocks, plane_count * pair_count * piece, channels // blocks), f32),
            pltpu.VMEM((total_lat, order_slots, total_lat), f32),
            pltpu.VMEM((low_each, total_lat, total_lat), bf16),
            pltpu.VMEM((high_each, high_each * plane_count, own_lats), bf16),
            pltpu.VMEM((total_lat, 2 * channels), bf16),
            pltpu.VMEM((low_each, total_lat, 2 * channels), bf16),
            pltpu.VMEM((2 * region, 2 * channels), f32),
            pltpu.VMEM((2 * region, 2 * channels), bf16),
            pltpu.VMEM((region, 2 * channels), bf16),
            pltpu.VMEM((2 * region, 2 * channels), bf16),
            pltpu.VMEM((row_count, lon_count, channels), f32),
            pltpu.VMEM((3, plane_count, piece, channels), bf16),
            pltpu.VMEM((3, plane_count, piece, channels), bf16),
            pltpu.VMEM((row_count, keys, channels), bf16),
            pltpu.VMEM((row_count, keys, channels), bf16),
            pltpu.VMEM((row_count, keys, channels), bf16),
            pltpu.VMEM((row_count, keys, channels), bf16),
            dma((7,)),
            dma((3, row_count)),
            dma((row_count, member_count - 1)),
            dma((row_count, member_count - 1)),
            dma((row_count, member_count - 1)),
            dma((row_count, member_count - 1)),
            dma((row_count,)),
            dma((row_count,)),
            dma((pair_count, 2, plane_count)),
            dma((pair_count, 2, plane_count)),
            dma((pair_count + 2, plane_count)),
            dma((pair_count + 2, plane_count)),
            dma((pair_count,)),
            dma((pair_count,)),
            dma((2,)),
            dma((2,)),
        ],
        compiler_params=pltpu.CompilerParams(
            collective_id=0, has_side_effects=True, vmem_limit_bytes=63 * 2**20
        ),
    )(
        grid_input[0],
        saved_mixed[0],
        target,
        land_weight,
        mix_weight,
        degree_gain,
        up_weight,
        down_weight,
        synth,
        analysis,
        start_log,
        cosine,
        quad,
        area,
    )
    return result[None]


def solution(mesh):
    in_specs = (
        P("member", "lat", None, None),
        P("member", "lat", None, None),
        P("lat", None, None),
        P("lat", None),
        P(),
        P(),
        P(),
        P(),
    )
    out_specs = P("member", "lat", None, None)
    return jax.shard_map(shards, mesh=mesh, in_specs=in_specs, out_specs=out_specs, check_vma=False)
```
